512 devices in a mesh: section: 8 (over z_hi, core), vocab: 64 (over z_lo, y, x).
Axes of the slice: x: 4, y: 8, z: 8 (z_hi: 4, z_lo: 2; z = z_hi * 2 + z_lo), core: 2. Of those that a mesh axis runs over, the one named last changes fastest.
Arguments:
- tap_hidden: bfloat16 [3, 320, 8192], P(None, 'section', 'vocab'), may hold values from -6 to 6
- join_weight: bfloat16 [3, 8192, 8192], P(None, 'vocab', 'section'), may hold values from -0.0390625 to 0.0390625
- norm_gain: float32 [8192], P('section'), may hold values from 0.1 to 1.9
- head_weight: bfloat16 [8192, 65536], P('section', 'vocab')
- target_logits: bfloat16 [320, 65536], P('section', 'vocab')
- seq_lengths: int32 [10], replicated, may hold values from 1 to 32, as said below
- seq_mask: int32 [10], replicated, may hold values 0 or 1
Outputs:
- draft_loss: float32 [], replicated
- join_grad: float32 [3, 8192, 8192], P(None, 'vocab', 'section')
- gain_grad: float32 [8192], P('section')
The draws below stay inside these ranges and needn't reach their ends.
Inputs may be any that keep to these rules, and one draw needn't show every extreme that they name: `seq_lengths`: one rollout of the window is live at all its 32 positions.
All inputs are finite; a program needn't handle non-finite values.
Results may differ from the reference program's by a relative error of at most 0.0059.
Values may be sent and summed in bfloat16 or wider, within the bound.
A program may use at most 64 MiB of HBM per device.

```python
import math
import jax
import jax.numpy as jnp
from jax import lax

D = 8192
TAPS = 3
TOKENS = 320
SPAN = 32
SEQS = 10
VOCAB = 65536


def draw_head_weight(key, part):
    key = jax.random.fold_in(key, 5)
    first_key = jax.random.fold_in(key, 0)
    spread = 3.0 / math.sqrt(D)
    values = spread * jax.random.normal(first_key, (D, VOCAB), jnp.float32)
    return values.astype(jnp.bfloat16)


def draw_target_logits(key, part):
    key = jax.random.fold_in(key, 11)
    first_key = jax.random.fold_in(key, 0)
    values = 3.0 * jax.random.normal(first_key, (TOKENS, VOCAB), jnp.float32)
    return values.astype(jnp.bfloat16)


def draw_seq_lengths(key, part):
    key = jax.random.fold_in(key, 3)
    first_key, second_key = jax.random.split(key, 2)
    values = jax.random.randint(first_key, (SEQS,), 1, SPAN + 1)
    full_one = jax.random.randint(second_key, (), 0, SEQS)
    return jnp.where(jnp.arange(SEQS, dtype=jnp.int32) == full_one, SPAN, values).astype(jnp.int32)


def touch_ends(values, own_key, least, top_value):
    place = [jax.random.randint(jax.random.fold_in(own_key, axis), (), 0, length) for axis, length in enumerate(values.shape)]
    widest = values.shape.index(max(values.shape))
    neighbour = place[:widest] + [(place[widest] + 1) % values.shape[widest]] + place[widest + 1:]
    return values.at[tuple(place)].set(least).at[tuple(neighbour)].set(top_value)


def block_levels(rng, extent, pieces, least, high):
    def one(dim, blocks):
        draws = jax.random.uniform(jax.random.fold_in(jax.random.fold_in(rng, 6), dim), (blocks,), jnp.float32, least / len(pieces), high / len(pieces))
        return jnp.repeat(jnp.exp(draws), extent[dim] // blocks).reshape((-1,) + (1,) * (len(extent) - dim - 1))

    factor_of = one(*pieces[0])
    for cut in pieces[1:]:
        factor_of = factor_of * one(*cut)
    return factor_of


def scatter_about(own_key, dims, deviation, bound, shards=(), kind=jnp.bfloat16):
    entries = deviation * jax.random.normal(own_key, dims, jnp.float32)
    if shards:
        entries = entries * block_levels(own_key, dims, shards, -0.22, 0.18)
    return jnp.clip(entries, -bound, bound).astype(kind)


def setup_inputs(seed: int = 0) -> dict:
    seeds = jax.random.split(jax.random.key(seed), 8)
    return {
        "tap_hidden": scatter_about(seeds[0], (TAPS, TOKENS, D), 1.0, 6.0, ((1, 8), (2, 64))),
        "join_weight": scatter_about(seeds[1], (TAPS, D, D), (TAPS * D) ** -0.5, 0.0390625, ((1, 64), (2, 8))),
        "norm_gain": jnp.clip(1.0 + 0.18 * jax.random.normal(seeds[2], (D,), jnp.float32), 0.1, 1.9),
        "head_weight": draw_head_weight(jax.random.fold_in(seeds[7], 71), 0),
        "target_logits": draw_target_logits(jax.random.fold_in(seeds[7], 71), 0),
        "seq_lengths": draw_seq_lengths(jax.random.fold_in(seeds[7], 71), 0),
        "seq_mask": touch_ends((jax.random.randint(seeds[6], (SEQS,), 0, 4) < 3).astype(jnp.int32), jax.random.fold_in(seeds[6], 1), 0, 1),
    }


LOSS_SCALE = 1024.0
EPS = 1e-05

def reference(tap_hidden, join_weight, norm_gain, head_weight, target_logits, seq_lengths, seq_mask):
    joined = jnp.dot(tap_hidden[0], join_weight[0], preferred_element_type=jnp.float32)
    for layer in range(1, TAPS):
        joined = joined + jnp.dot(tap_hidden[layer], join_weight[layer], preferred_element_type=jnp.float32)
    square_sum = lax.optimization_barrier(jnp.sum(joined * joined, axis=1, keepdims=True))
    inverse = lax.rsqrt(square_sum / D + EPS)
    normed = (joined * inverse * norm_gain[None, :]).astype(jnp.bfloat16)
    draft = jnp.dot(normed, head_weight, preferred_element_type=jnp.float32)
    target = target_logits.astype(jnp.float32)
    draft_peak = lax.optimization_barrier(jnp.max(draft, axis=1, keepdims=True))
    draft_lse = draft_peak + jnp.log(lax.optimization_barrier(jnp.sum(jnp.exp(draft - draft_peak), axis=1, keepdims=True)))
    target_peak = lax.optimization_barrier(jnp.max(target, axis=1, keepdims=True))
    target_exp = jnp.exp(target - target_peak)
    target_sum = lax.optimization_barrier(jnp.sum(target_exp, axis=1, keepdims=True))
    target_lse = target_peak + jnp.log(target_sum)
    cross = lax.optimization_barrier(jnp.sum(target_exp * (target - draft), axis=1, keepdims=True))
    divergence = cross / target_sum - target_lse + draft_lse
    position = jnp.arange(TOKENS, dtype=jnp.int32)
    sequence = position // SPAN
    offset = position % SPAN
    length = seq_lengths[sequence]
    keep = seq_mask[sequence]
    weight = jnp.where(offset < length, keep.astype(jnp.float32) / (length.astype(jnp.float32) * SEQS), 0.0)[:, None]
    draft_loss = jnp.sum(weight * divergence)
    dlogit = (LOSS_SCALE * weight * (jnp.exp(draft - draft_lse) - target_exp / target_sum)).astype(jnp.bfloat16)
    dnormed = lax.dot_general(dlogit, head_weight, (((1,), (1,)), ((), ())), preferred_element_type=jnp.float32)
    gain_grad = lax.optimization_barrier(jnp.sum(dnormed * joined * inverse, axis=0))
    scaled = dnormed * norm_gain[None, :]
    inner = lax.optimization_barrier(jnp.sum(scaled * joined, axis=1, keepdims=True))
    dfused = (scaled * inverse - joined * inner * inverse ** 3 / D).astype(jnp.bfloat16)
    grads = [jnp.dot(tap_hidden[layer].T, dfused, preferred_element_type=jnp.float32) for layer in range(TAPS)]
    join_grad = jnp.stack(grads, axis=0)
    return (draft_loss, join_grad, gain_grad)
```

```python
import jax
import jax.numpy as jnp
from jax import lax
from jax.experimental import pallas as pl
from jax.experimental.pallas import tpu as pltpu
from jax.sharding import PartitionSpec as P

MESH = pl.DeviceIdType.MESH
F32 = jnp.float32
BF16 = jnp.bfloat16

SPAN = 32
SEQS = 10
LOSS_SCALE = 1024.0
EPS = 1e-05
WIDTH = 8192
TAPS = 3
BLK = 40
TOK = 320
COL = 128
LOC = 1024


def fold(a):
    return jnp.concatenate([a[:, : LOC // 2], a[:, LOC // 2 :]], axis=0)


def unfold(a):
    return jnp.concatenate([a[:BLK], a[BLK:]], axis=1)


LEVELS = 32767.0
BOUND = TAPS * COL * 6.0 * 0.0390625


def pack(low, high):
    low = jnp.where(low < 0, low - 0.5, low + 0.5).astype(jnp.int32)
    high = jnp.where(high < 0, high - 0.5, high + 0.5).astype(jnp.int32)
    return (high << 16) | (low & 0xFFFF)


def unpack(word):
    return ((word << 16) >> 16).astype(F32), (word >> 16).astype(F32)


def root_code(a):
    root = jnp.sqrt(jnp.sqrt(jnp.minimum(jnp.abs(a) * (1.0 / BOUND), 1.0))) * LEVELS
    return jnp.where(a < 0, -root, root)


def root_value(code):
    code = code * (1.0 / LEVELS)
    return BOUND * (code * code) * (code * jnp.abs(code))


def both(a):
    return jnp.concatenate([a, a], axis=0)


def columns_to_rows(columns):
    lane = lax.broadcasted_iota(jnp.int32, (BLK, 128), 1)
    out = jnp.zeros((BLK, 128), F32)
    for i, column in enumerate(columns):
        out = jnp.where(lane == i, column, out)
    out = jnp.concatenate([out, jnp.zeros((128 - BLK, 128), F32)], axis=0)
    return out.T[:8]


def stack_rows(rows):
    sub = lax.broadcasted_iota(jnp.int32, (8, 128), 0)
    out = jnp.zeros((8, 128), F32)
    for i, row in enumerate(rows):
        out = jnp.where(sub == i, row, out)
    return out


def rows_to_columns(rows):
    return jnp.concatenate([rows, jnp.zeros((120, 128), F32)], axis=0).T


def merge_stats(parts):
    top_d, top_t = parts[0][0:1], parts[0][3:4]
    for p in parts[1:]:
        top_d = jnp.maximum(top_d, p[0:1])
        top_t = jnp.maximum(top_t, p[3:4])
    sums = [jnp.zeros((1, 128), F32) for _ in range(5)]
    for p in parts:
        a = jnp.exp(p[0:1] - top_d)
        b = jnp.exp(p[3:4] - top_t)
        sums[0] += a * p[1:2]
        sums[1] += a * p[2:3]
        sums[2] += b * p[4:5]
        sums[3] += b * p[5:6]
        sums[4] += b * p[6:7]
    return [top_d, sums[0], sums[1], top_t, sums[2], sums[3], sums[4]]


def kernel(
    tap_ref, jw_ref, gain_ref, head_ref, tl_ref, len_ref, mask_ref,
    loss_ref, jg_ref, gg_ref,
    tapg, tapl, sb1, rb1, a1, b1, p1, jy, sqx, ub, ul, cs, cr, ds, own, zs, zr, zss, zsr, sqb, invc,
    st0, st1, st2, dlb, dl, qb, sb2, rb2, a2, b2, p2, dn, df, ggb, dfl,
    s_tap, r_tap, s_x1, r_x1, s_y1, r_y1, s_g1, r_g1, s_sx, r_sx, s_u, r_u, s_c, r_c, s_z, r_z, s_zs, r_zs,
    s_sq, r_sq,
    s_s1, r_s1, s_s2, r_s2, s_dl, r_dl, s_fw, s_q, r_q, s_x2, r_x2, s_y2, r_y2, s_g2, r_g2,
    s_df, r_df, s_gg, r_gg,
):
    sec = lax.axis_index("section")
    voc = lax.axis_index("vocab")
    zh, c = lax.div(sec, 2), lax.rem(sec, 2)
    zl, y, x = lax.div(voc, 32), lax.rem(lax.div(voc, 4), 8), lax.rem(voc, 4)
    j = zl * 4 + x
    pi = c * 4 + zh

    sec_peers = []
    for a, b in ((2, 0), (2, 1), (1, 0), (3, 0), (1, 1), (3, 1), (0, 1)):
        zh2, c2 = lax.rem(zh + a, 4), lax.rem(c + b, 2)
        sec_peers.append((c2 * 4 + zh2, (zh2 * 2 + c2, voc)))
    zh_peers = []
    for a in (2, 1, 3):
        zh2 = lax.rem(zh + a, 4)
        zh_peers.append((zh2, (zh2 * 2 + c, voc)))
    core_dev = (zh * 2 + (1 - c), voc)
    xz_peers = []
    for a, b in ((1, 2), (1, 1), (1, 3), (0, 2), (0, 1), (0, 3), (1, 0)):
        zl2, x2 = lax.rem(zl + a, 2), lax.rem(x + b, 4)
        xz_peers.append((zl2 * 4 + x2, (sec, zl2 * 32 + y * 4 + x2)))
    y_peers = []
    for a in (4, 3, 5, 2, 6, 1, 7):
        y2 = lax.rem(y + a, 8)
        y_peers.append((y2, (sec, zl * 32 + y2 * 4 + x)))

    barrier = pltpu.get_barrier_semaphore()
    for _, dev in sec_peers + xz_peers + y_peers:
        pl.semaphore_signal(barrier, inc=1, device_id=dev, device_id_type=MESH)
    pl.semaphore_wait(barrier, 21)

    pending = []

    def send(src, dst, s_sem, r_sem, dev):
        copy = pltpu.make_async_remote_copy(src, dst, s_sem, r_sem, device_id=dev, device_id_type=MESH)
        copy.start()
        pending.append(copy)

    def send_all(peers, src, dst, s_sem, r_sem, slot):
        for k, (other, dev) in enumerate(peers):
            send(src(other), dst.at[slot], s_sem.at[k], r_sem.at[slot], dev)

    def arrived(dst, s_sem, r_sem, dev):
        pltpu.make_async_remote_copy(dst, dst, s_sem, r_sem, device_id=dev, device_id_type=MESH).wait_recv()

    def wait_all(peers, dst, s_sem, r_sem):
        for k, (other, dev) in enumerate(peers):
            arrived(dst.at[other], s_sem.at[k], r_sem.at[other], dev)

    send_all(sec_peers, lambda other: tap_ref, tapg, s_tap, r_tap, pi)
    tapg[pi] = tap_ref[...]
    wait_all(sec_peers, tapg, s_tap, r_tap)
    blocks = [tapg[p].astype(F32) for p in range(8)]
    for k in range(TAPS):
        rows = jnp.concatenate([b[k * BLK : (k + 1) * BLK] for b in blocks], axis=0)
        tapl[:, k * COL : (k + 1) * COL] = rows.astype(BF16)

    def join_step(i, carry):
        at = pl.ds(pl.multiple_of(i * 256, 256), 256)
        acc = jnp.dot(tapl[...], jw_ref[:, at], preferred_element_type=F32)
        acc = root_code(acc)
        sb1[2 * i] = pack(acc[:160, :COL], acc[160:, :COL])
        sb1[2 * i + 1] = pack(acc[:160, COL:], acc[160:, COL:])
        return carry

    lax.fori_loop(0, 4, join_step, 0)

    def from_roots(rb):
        low, high = [root_value(half) for half in unpack(rb[0])]
        for k in range(1, 8):
            more = [root_value(half) for half in unpack(rb[k])]
            low, high = low + more[0], high + more[1]
        return jnp.concatenate([low, high], axis=0)

    def from_bf16(rb):
        total = rb[0].astype(F32)
        for k in range(1, 8):
            total += rb[k].astype(F32)
        return total

    def vocab_sum(collect, sb, rb, a_buf, b_buf, p_buf, out, s_x, r_x, s_y, r_y, s_g, r_g):
        send_all(xz_peers, lambda other: sb.at[other], rb, s_x, r_x, j)
        rb[j] = sb[j]
        wait_all(xz_peers, rb, s_x, r_x)
        total = collect(rb)
        for k in range(8):
            a_buf[k] = total[k * BLK : (k + 1) * BLK]
        send_all(y_peers, lambda other: a_buf.at[other], b_buf, s_y, r_y, y)
        b_buf[y] = a_buf[y]
        wait_all(y_peers, b_buf, s_y, r_y)
        piece = b_buf[0]
        for k in range(1, 8):
            piece += b_buf[k]
        p_buf[...] = piece
        send_all(y_peers, lambda other: p_buf, out, s_g, r_g, y)
        out[y] = piece
        wait_all(y_peers, out, s_g, r_g)

    vocab_sum(from_roots, sb1, rb1, a1, b1, p1, jy, s_x1, r_x1, s_y1, r_y1, s_g1, r_g1)

    joined = jnp.concatenate([jy[k] for k in range(8)], axis=0)
    square = jnp.concatenate([joined * joined, jnp.zeros((64, COL), F32)], axis=0)
    sqx[j] = jnp.sum(square.T, axis=0, keepdims=True)
    send_all(xz_peers, lambda other: sqx.at[j], sqx, s_sx, r_sx, j)
    code = joined * (LEVELS * lax.rsqrt(jnp.maximum(jnp.sum(square[:TOK], axis=1, keepdims=True), 1e-30)))
    ub[j] = pack(code[:160], code[160:])
    send_all(xz_peers, lambda other: ub.at[j], ub, s_u, r_u, j)
    wait_all(xz_peers, sqx, s_sx, r_sx)
    square = sqx[0]
    for k in range(1, 8):
        square += sqx[k]
    sqb[pi] = square
    send_all(sec_peers, lambda other: sqb.at[pi], sqb, s_sq, r_sq, pi)
    wait_all(sec_peers, sqb, s_sq, r_sq)
    square = sqb[0]
    for k in range(1, 8):
        square += sqb[k]
    inverse = lax.rsqrt(square / WIDTH + EPS)
    factors = [jnp.sqrt(sqx[k]) * (1.0 / LEVELS) * inverse for k in range(8)]
    factors = jnp.concatenate(factors + [jnp.zeros((120, 384), F32)], axis=0).T
    inverse = jnp.broadcast_to(inverse, (128, 384)).T
    for k in range(8):
        invc[k] = inverse[k * BLK : (k + 1) * BLK]
    wait_all(xz_peers, ub, s_u, r_u)
    for k in range(8):
        for h, half in enumerate(unpack(ub[k])):
            normed = half * factors[h * 160 : (h + 1) * 160, k : k + 1] * gain_ref[k : k + 1, :]
            ul[h, :, k * COL : (k + 1) * COL] = normed.astype(BF16)

    def draft_half(half, out):
        def step(i, carry):
            at = pl.ds(pl.multiple_of(i * 256, 256), 256)
            out[:, at] = jnp.dot(ul[half], head_ref[:, at], preferred_element_type=F32)
            return carry

        lax.fori_loop(0, 4, step, 0)

    draft_half(1 - c, cs)
    send(cs, cr, s_c, r_c, core_dev)

    draft_half(c, ds)
    arrived(cr, s_c, r_c, core_dev)
    tops = []
    for k in range(4):
        rows = slice(k * BLK, (k + 1) * BLK)
        part = ds[rows, :] + cr[rows, :]
        ds[rows, :] = part
        tops.append(jnp.maximum(jnp.max(jnp.abs(part), axis=1, keepdims=True), 1e-30))
        code = part * (LEVELS / tops[-1])
        zs[k] = pack(code[:, : LOC // 2], code[:, LOC // 2 :])
    zss[...] = columns_to_rows(tops)
    for k, (other, dev) in enumerate(zh_peers):
        send(zss, zsr.at[zh], s_zs.at[k], r_zs.at[zh], dev)
        send(zs.at[other], zr.at[zh], s_z.at[k], r_z.at[zh], dev)
    zsr[zh] = zss[...]
    own[...] = fold(ds[pl.ds(pl.multiple_of(zh * BLK, 8), BLK), :])
    target = fold(tl_ref[...].astype(F32))

    lane = lax.broadcasted_iota(jnp.int32, (1, 128), 1)
    position = sec * BLK + lane
    sequence = position // SPAN
    offset = position % SPAN
    length = jnp.zeros((1, 128), jnp.int32)
    keep = jnp.zeros((1, 128), jnp.int32)
    for q in range(SEQS):
        length = jnp.where(sequence == q, len_ref[q], length)
        keep = jnp.where(sequence == q, mask_ref[q], keep)
    live = (offset < length) & (lane < BLK)
    weight = jnp.where(live, keep.astype(F32) / (jnp.maximum(length, 1).astype(F32) * SEQS), 0.0)

    wait_all(zh_peers, zsr, s_zs, r_zs)
    steps = rows_to_columns(stack_rows([zsr[other, pl.ds(zh, 1), :] for other, _ in zh_peers])) * (1.0 / LEVELS)
    draft = own[...]
    for k, (other, dev) in enumerate(zh_peers):
        arrived(zr.at[other], s_z.at[k], r_z.at[other], dev)
        draft += jnp.concatenate(unpack(zr[other]), axis=0) * both(steps[:BLK, k : k + 1])

    def per_token(a, op, reduce):
        m = op(op(a[:, :128], a[:, 128:256]), op(a[:, 256:384], a[:, 384:]))
        return reduce(op(m[:BLK], m[BLK:]), axis=1, keepdims=True)

    def top(a):
        return per_token(a, jnp.maximum, jnp.max)

    def add(a):
        return per_token(a, jnp.add, jnp.sum)

    d_top = top(draft)
    d_exp = jnp.exp(draft - both(d_top))
    t_top = top(target)
    t_exp = jnp.exp(target - both(t_top))
    st0[...] = columns_to_rows(
        [d_top, add(d_exp), add(d_exp * draft), t_top, add(t_exp), add(t_exp * (target - draft)), add(t_exp * draft)]
    )
    send_all(xz_peers, lambda other: st0, st1, s_s1, r_s1, j)
    st1[j] = st0[...]
    wait_all(xz_peers, st1, s_s1, r_s1)
    st2[y] = stack_rows(merge_stats([st1[k] for k in range(8)]))
    send_all(y_peers, lambda other: st2.at[y], st2, s_s2, r_s2, y)
    wait_all(y_peers, st2, s_s2, r_s2)
    d_top, d_sum, d_first, t_top, t_sum, cross, t_first = merge_stats([st2[k] for k in range(8)])
    valid = lane < BLK
    d_sum = jnp.where(valid, d_sum, 1.0)
    t_sum = jnp.where(valid, t_sum, 1.0)
    d_lse = d_top + jnp.log(d_sum)
    t_lse = t_top + jnp.log(t_sum)
    loss = weight * (cross / t_sum - t_lse + d_lse)
    scale = LOSS_SCALE * weight
    along = scale * (d_first / d_sum - t_first / t_sum)

    cols = rows_to_columns(stack_rows([d_lse, scale, t_top, scale / t_sum]))
    dlogit = both(cols[:BLK, 1:2]) * jnp.exp(draft - both(cols[:BLK, 0:1])) - both(cols[:BLK, 3:4]) * jnp.exp(
        target - both(cols[:BLK, 2:3])
    )
    dlb[pi] = dlogit.astype(BF16)
    for k, (other, dev) in enumerate(zh_peers):
        send(dlb.at[pi], dlb.at[pi], s_dl.at[k], r_dl.at[pi], dev)
    send(dlb.at[pi], dlb.at[pi], s_fw.at[3], r_dl.at[pi], core_dev)
    qb[pi] = stack_rows([along, loss])
    send_all(sec_peers, lambda other: qb.at[pi], qb, s_q, r_q, pi)
    for k, (other, dev) in enumerate(zh_peers[1:] + zh_peers[:1]):
        slot = c * 4 + other
        arrived(dlb.at[slot], s_dl.at[k], r_dl.at[slot], dev)
        send(dlb.at[slot], dlb.at[slot], s_fw.at[k], r_dl.at[slot], core_dev)

    def grad_half(half):
        for k in range(0, 4, 2):
            pair = [unfold(dlb[half * 4 + k + i].astype(F32)) for i in range(2)]
            dl[half, k * BLK : (k + 2) * BLK] = jnp.concatenate(pair, axis=0).astype(BF16)

        def step(i, carry):
            at = pl.ds(pl.multiple_of(i * 256, 256), 256)
            acc = lax.dot_general(
                dl[half], head_ref[at, :], (((1,), (1,)), ((), ())), preferred_element_type=F32
            )
            rows = pl.ds(pl.multiple_of(half * 160, 16), 160)
            sb2[2 * i, rows] = acc[:, :COL].astype(BF16)
            sb2[2 * i + 1, rows] = acc[:, COL:].astype(BF16)
            return carry

        lax.fori_loop(0, 4, step, 0)

    grad_half(c)
    for zh2 in range(4):
        slot = (1 - c) * 4 + zh2
        arrived(dlb.at[slot], s_fw.at[0], r_dl.at[slot], core_dev)
    grad_half(1 - c)

    vocab_sum(from_bf16, sb2, rb2, a2, b2, p2, dn, s_x2, r_x2, s_y2, r_y2, s_g2, r_g2)

    wait_all(sec_peers, qb, s_q, r_q)
    loss = qb[0, 1:2]
    for k in range(1, 8):
        loss += qb[k, 1:2]
    loss_ref[0, 0] = jnp.sum(loss)
    q_cols = rows_to_columns(stack_rows([qb[k, 0:1] for k in range(8)]))
    gain = gain_ref[pl.ds(j, 1), :]
    gg = jnp.zeros((BLK, COL), F32)
    pair = []
    for k in range(8):
        inv = invc[k]
        joined = jy[k]
        grad = dn[k] * inv
        gg += grad * joined
        pair.append(grad * gain - joined * (q_cols[:BLK, k : k + 1] * inv * inv / WIDTH))
        if k % 2:
            df[j, (k - 1) * BLK : (k + 1) * BLK] = jnp.concatenate(pair, axis=0).astype(BF16)
            pair = []
    send_all(xz_peers, lambda other: df.at[j], df, s_df, r_df, j)
    ggb[j] = jnp.sum(gg, axis=0, keepdims=True)
    send_all(xz_peers, lambda other: ggb.at[j], ggb, s_gg, r_gg, j)
    wait_all(xz_peers, df, s_df, r_df)
    for k in range(8):
        dfl[:, k * COL : (k + 1) * COL] = df[k]

    def out_step(i, carry):
        at = pl.ds(pl.multiple_of(i * 256, 256), 256)
        for k in range(TAPS):
            jg_ref[k * COL : (k + 1) * COL, at] = lax.dot_general(
                tapl[:, k * COL : (k + 1) * COL], dfl[:, at], (((0,), (0,)), ((), ())), preferred_element_type=F32
            )
        return carry

    lax.fori_loop(0, 4, out_step, 0)
    wait_all(xz_peers, ggb, s_gg, r_gg)
    for k in range(8):
        gg_ref[k : k + 1, :] = ggb[k]
    for copy in pending:
        copy.wait_send()


def shards(tap_hidden, join_weight, norm_gain, head_weight, target_logits, seq_lengths, seq_mask):
    taps = jnp.pad(tap_hidden.reshape(TAPS * BLK, COL), ((0, 128 - TAPS * BLK), (0, 0)))
    vmem = pl.BlockSpec(memory_space=pltpu.VMEM)
    smem = pl.BlockSpec(memory_space=pltpu.SMEM)
    dma = pltpu.SemaphoreType.DMA
    V = pltpu.VMEM
    scratch = [
        V((8, 128, COL), BF16), V((TOK, TAPS * COL), BF16),
        V((8, TOK // 2, COL), jnp.int32), V((8, TOK // 2, COL), jnp.int32),
        V((8, BLK, COL), F32), V((8, BLK, COL), F32), V((BLK, COL), F32), V((8, BLK, COL), F32),
        V((8, 1, 384), F32), V((8, TOK // 2, COL), jnp.int32), V((2, TOK // 2, LOC), BF16),
        V((TOK // 2, LOC), F32), V((TOK // 2, LOC), F32), V((TOK // 2, LOC), F32),
        V((2 * BLK, LOC // 2), F32),
        V((4, BLK, LOC // 2), jnp.int32), V((4, BLK, LOC // 2), jnp.int32), V((8, 128), F32), V((4, 8, 128), F32),
        V((8, 1, 384), F32), V((8, BLK, COL), F32),
        V((8, 128), F32), V((8, 8, 128), F32), V((8, 8, 128), F32),
        V((8, 2 * BLK, LOC // 2), BF16), V((2, TOK // 2, LOC), BF16), V((8, 8, 128), F32),
        V((8, TOK, COL), BF16), V((8, TOK, COL), BF16),
        V((8, BLK, COL), F32), V((8, BLK, COL), F32), V((BLK, COL), F32), V((8, BLK, COL), F32),
        V((8, TOK, COL), BF16), V((8, 1, COL), F32), V((TOK, LOC), BF16),
        dma((7,)), dma((8,)),
        dma((7,)), dma((8,)), dma((7,)), dma((8,)), dma((7,)), dma((8,)),
        dma((7,)), dma((8,)), dma((7,)), dma((8,)),
        dma, dma,
        dma((3,)), dma((4,)), dma((3,)), dma((4,)),
        dma((7,)), dma((8,)),
        dma((7,)), dma((8,)), dma((7,)), dma((8,)),
        dma((3,)), dma((8,)), dma((4,)),
        dma((7,)), dma((8,)),
        dma((7,)), dma((8,)), dma((7,)), dma((8,)), dma((7,)), dma((8,)),
        dma((7,)), dma((8,)), dma((7,)), dma((8,)),
    ]
    loss, join_grad, gain_grad = pl.pallas_call(
        kernel,
        out_shape=(
            jax.ShapeDtypeStruct((1, 1), F32),
            jax.ShapeDtypeStruct((TAPS * COL, LOC), F32),
            jax.ShapeDtypeStruct((8, COL), F32),
        ),
        in_specs=[vmem] * 5 + [smem] * 2,
        out_specs=(smem, vmem, vmem),
        scratch_shapes=scratch,
        compiler_params=pltpu.CompilerParams(
            collective_id=0, has_side_effects=True, vmem_limit_bytes=48 * 1024 * 1024
        ),
        name="draft_step",
    )(
        taps,
        join_weight.reshape(TAPS * COL, LOC),
        norm_gain.reshape(8, COL),
        head_weight,
        target_logits,
        seq_lengths,
        seq_mask,
    )
    return loss.reshape(()), join_grad.reshape(TAPS, COL, LOC), gain_grad.reshape(LOC)


def solution(mesh):
    in_specs = (
        P(None, "section", "vocab"),
        P(None, "vocab", "section"),
        P("section"),
        P("section", "vocab"),
        P("section", "vocab"),
        P(),
        P(),
    )
    out_specs = (P(), P(None, "vocab", "section"), P("section"))
    return jax.shard_map(shards, mesh=mesh, in_specs=in_specs, out_specs=out_specs, check_vma=False)
```

```python
import jax
import jax.numpy as jnp
from jax import lax
from jax.experimental import pallas as pl
from jax.experimental.pallas import tpu as pltpu
from jax.sharding import PartitionSpec as P

MESH = pl.DeviceIdType.MESH
F32 = jnp.float32
BF16 = jnp.bfloat16

SPAN = 32
SEQS = 10
LOSS_SCALE = 1024.0
EPS = 1e-05
WIDTH = 8192
TAPS = 3
BLK = 40
TOK = 320
COL = 128
LOC = 1024


def fold(a):
    return jnp.concatenate([a[:, : LOC // 2], a[:, LOC // 2 :]], axis=0)


def unfold(a):
    return jnp.concatenate([a[:BLK], a[BLK:]], axis=1)


LEVELS = 32767.0
BOUND = TAPS * COL * 6.0 * 0.0390625


def pack(low, high):
    low = jnp.where(low < 0, low - 0.5, low + 0.5).astype(jnp.int32)
    high = jnp.where(high < 0, high - 0.5, high + 0.5).astype(jnp.int32)
    return (high << 16) | (low & 0xFFFF)


def unpack(word):
    return ((word << 16) >> 16).astype(F32), (word >> 16).astype(F32)


def root_code(a):
    root = jnp.sqrt(jnp.sqrt(jnp.minimum(jnp.abs(a) * (1.0 / BOUND), 1.0))) * LEVELS
    return jnp.where(a < 0, -root, root)


def root_value(code):
    code = code * (1.0 / LEVELS)
    return BOUND * (code * code) * (code * jnp.abs(code))


def both(a):
    return jnp.concatenate([a, a], axis=0)


def columns_to_rows(columns):
    lane = lax.broadcasted_iota(jnp.int32, (BLK, 128), 1)
    out = jnp.zeros((BLK, 128), F32)
    for i, column in enumerate(columns):
        out = jnp.where(lane == i, column, out)
    out = jnp.concatenate([out, jnp.zeros((128 - BLK, 128), F32)], axis=0)
    return out.T[:8]


def stack_rows(rows):
    sub = lax.broadcasted_iota(jnp.int32, (8, 128), 0)
    out = jnp.zeros((8, 128), F32)
    for i, row in enumerate(rows):
        out = jnp.where(sub == i, row, out)
    return out


def rows_to_columns(rows):
    return jnp.concatenate([rows, jnp.zeros((120, 128), F32)], axis=0).T


def merge_stats(parts):
    top_d, top_t = parts[0][0:1], parts[0][3:4]
    for p in parts[1:]:
        top_d = jnp.maximum(top_d, p[0:1])
        top_t = jnp.maximum(top_t, p[3:4])
    sums = [jnp.zeros((1, 128), F32) for _ in range(5)]
    for p in parts:
        a = jnp.exp(p[0:1] - top_d)
        b = jnp.exp(p[3:4] - top_t)
        sums[0] += a * p[1:2]
        sums[1] += a * p[2:3]
        sums[2] += b * p[4:5]
        sums[3] += b * p[5:6]
        sums[4] += b * p[6:7]
    return [top_d, sums[0], sums[1], top_t, sums[2], sums[3], sums[4]]


def kernel(
    tap_hbm, jw_hbm, gain_hbm, head_hbm, tl_hbm, len_hbm, mask_hbm,
    loss_ref, jg_ref, gg_ref,
    tap_ref, jw_ref, gain_ref, head_ref, tl_ref, len_ref, mask_ref,
    tapg, tapl, sb1, rb1, a1, b1, p1, jy, sqx, ub, ul, cs, cr, ds, own, zs, zr, zss, zsr, sqb, invc,
    st0, st1, st2, dlb, dl, qb, sb2, rb2, a2, b2, p2, dn, df, ggb, dfl,
    s_in, s_tap, r_tap, s_tf, s_x1, r_x1, s_y1, r_y1, s_g1, r_g1, s_sx, r_sx, s_u, r_u, s_c, r_c, s_z, r_z, s_zs, r_zs,
    s_sq, r_sq,
    s_s1, r_s1, s_s2, r_s2, s_dl, r_dl, s_fw, s_q, r_q, s_x2, r_x2, s_y2, r_y2, s_g2, r_g2,
    s_df, r_df, s_gg, r_gg,
):
    sec = lax.axis_index("section")
    voc = lax.axis_index("vocab")
    zh, c = lax.div(sec, 2), lax.rem(sec, 2)
    zl, y, x = lax.div(voc, 32), lax.rem(lax.div(voc, 4), 8), lax.rem(voc, 4)
    j = zl * 4 + x
    pi = c * 4 + zh

    sec_peers = []
    for a, b in ((2, 0), (2, 1), (1, 0), (3, 0), (1, 1), (3, 1), (0, 1)):
        zh2, c2 = lax.rem(zh + a, 4), lax.rem(c + b, 2)
        sec_peers.append((c2 * 4 + zh2, (zh2 * 2 + c2, voc)))
    zh_peers = []
    for a in (2, 1, 3):
        zh2 = lax.rem(zh + a, 4)
        zh_peers.append((zh2, (zh2 * 2 + c, voc)))
    core_dev = (zh * 2 + (1 - c), voc)
    xz_peers = []
    for a, b in ((1, 2), (1, 1), (1, 3), (0, 2), (0, 1), (0, 3), (1, 0)):
        zl2, x2 = lax.rem(zl + a, 2), lax.rem(x + b, 4)
        xz_peers.append((zl2 * 4 + x2, (sec, zl2 * 32 + y * 4 + x2)))
    y_peers = []
    for a in (4, 3, 5, 2, 6, 1, 7):
        y2 = lax.rem(y + a, 8)
        y_peers.append((y2, (sec, zl * 32 + y2 * 4 + x)))

    inputs = (
        (tap_hbm, tap_ref), (jw_hbm, jw_ref), (gain_hbm, gain_ref), (len_hbm, len_ref), (mask_hbm, mask_ref),
        (head_hbm, head_ref), (tl_hbm, tl_ref),
    )
    loads = [pltpu.make_async_copy(src, dst, s_in.at[i]) for i, (src, dst) in enumerate(inputs)]
    for load in loads:
        load.start()

    barrier = pltpu.get_barrier_semaphore()
    for _, dev in sec_peers + xz_peers + y_peers:
        pl.semaphore_signal(barrier, inc=1, device_id=dev, device_id_type=MESH)
    loads[0].wait()
    taps = [tap_ref[k].astype(F32) for k in range(TAPS)] + [jnp.zeros((128 - TAPS * BLK, COL), F32)]
    tapg[pi] = jnp.concatenate(taps, axis=0).astype(BF16)
    pl.semaphore_wait(barrier, 21)

    pending = []

    def send(src, dst, s_sem, r_sem, dev):
        copy = pltpu.make_async_remote_copy(src, dst, s_sem, r_sem, device_id=dev, device_id_type=MESH)
        copy.start()
        pending.append(copy)

    def send_all(peers, src, dst, s_sem, r_sem, slot):
        for k, (other, dev) in enumerate(peers):
            send(src(other), dst.at[slot], s_sem.at[k], r_sem.at[slot], dev)

    def arrived(dst, s_sem, r_sem, dev):
        pltpu.make_async_remote_copy(dst, dst, s_sem, r_sem, device_id=dev, device_id_type=MESH).wait_recv()

    def wait_all(peers, dst, s_sem, r_sem):
        for k, (other, dev) in enumerate(peers):
            arrived(dst.at[other], s_sem.at[k], r_sem.at[other], dev)

    for k, (other, dev) in enumerate(zh_peers):
        send(tapg.at[pi], tapg.at[pi], s_tap.at[k], r_tap.at[pi], dev)
    send(tapg.at[pi], tapg.at[pi], s_tf.at[3], r_tap.at[pi], core_dev)
    for k, (other, dev) in enumerate(zh_peers[1:] + zh_peers[:1]):
        slot = c * 4 + other
        arrived(tapg.at[slot], s_tap.at[k], r_tap.at[slot], dev)
        send(tapg.at[slot], tapg.at[slot], s_tf.at[k], r_tap.at[slot], core_dev)
    for load in loads[1:]:
        load.wait()
    for zh2 in range(4):
        slot = (1 - c) * 4 + zh2
        arrived(tapg.at[slot], s_tf.at[0], r_tap.at[slot], core_dev)
    blocks = [tapg[p].astype(F32) for p in range(8)]
    for k in range(TAPS):
        rows = jnp.concatenate([b[k * BLK : (k + 1) * BLK] for b in blocks], axis=0)
        tapl[:, k * COL : (k + 1) * COL] = rows.astype(BF16)

    def join_step(i, carry):
        at = pl.ds(pl.multiple_of(i * 256, 256), 256)
        acc = jnp.dot(tapl[...], jw_ref[:, at], preferred_element_type=F32)
        acc = root_code(acc)
        sb1[2 * i] = pack(acc[:160, :COL], acc[160:, :COL])
        sb1[2 * i + 1] = pack(acc[:160, COL:], acc[160:, COL:])
        return carry

    lax.fori_loop(0, 4, join_step, 0)

    def from_roots(rb):
        low, high = [root_value(half) for half in unpack(rb[0])]
        for k in range(1, 8):
            more = [root_value(half) for half in unpack(rb[k])]
            low, high = low + more[0], high + more[1]
        return jnp.concatenate([low, high], axis=0)

    def from_bf16(rb):
        total = rb[0].astype(F32)
        for k in range(1, 8):
            total += rb[k].astype(F32)
        return total

    def vocab_sum(collect, sb, rb, a_buf, b_buf, p_buf, out, s_x, r_x, s_y, r_y, s_g, r_g):
        send_all(xz_peers, lambda other: sb.at[other], rb, s_x, r_x, j)
        rb[j] = sb[j]
        wait_all(xz_peers, rb, s_x, r_x)
        total = collect(rb)
        for k in range(8):
            a_buf[k] = total[k * BLK : (k + 1) * BLK]
        send_all(y_peers, lambda other: a_buf.at[other], b_buf, s_y, r_y, y)
        b_buf[y] = a_buf[y]
        wait_all(y_peers, b_buf, s_y, r_y)
        piece = b_buf[0]
        for k in range(1, 8):
            piece += b_buf[k]
        p_buf[...] = piece
        send_all(y_peers, lambda other: p_buf, out, s_g, r_g, y)
        out[y] = piece
        wait_all(y_peers, out, s_g, r_g)

    vocab_sum(from_roots, sb1, rb1, a1, b1, p1, jy, s_x1, r_x1, s_y1, r_y1, s_g1, r_g1)

    joined = jnp.concatenate([jy[k] for k in range(8)], axis=0)
    square = jnp.concatenate([joined * joined, jnp.zeros((64, COL), F32)], axis=0)
    sqx[j] = jnp.sum(square.T, axis=0, keepdims=True)
    send_all(xz_peers, lambda other: sqx.at[j], sqx, s_sx, r_sx, j)
    code = joined * (LEVELS * lax.rsqrt(jnp.maximum(jnp.sum(square[:TOK], axis=1, keepdims=True), 1e-30)))
    ub[j] = pack(code[:160], code[160:])
    send_all(xz_peers, lambda other: ub.at[j], ub, s_u, r_u, j)
    wait_all(xz_peers, sqx, s_sx, r_sx)
    square = sqx[0]
    for k in range(1, 8):
        square += sqx[k]
    sqb[pi] = square
    send_all(sec_peers, lambda other: sqb.at[pi], sqb, s_sq, r_sq, pi)
    wait_all(sec_peers, sqb, s_sq, r_sq)
    square = sqb[0]
    for k in range(1, 8):
        square += sqb[k]
    inverse = lax.rsqrt(square / WIDTH + EPS)
    factors = [jnp.sqrt(sqx[k]) * (1.0 / LEVELS) * inverse for k in range(8)]
    factors = jnp.concatenate(factors + [jnp.zeros((120, 384), F32)], axis=0).T
    inverse = jnp.broadcast_to(inverse, (128, 384)).T
    for k in range(8):
        invc[k] = inverse[k * BLK : (k + 1) * BLK]
    wait_all(xz_peers, ub, s_u, r_u)
    for k in range(8):
        for h, half in enumerate(unpack(ub[k])):
            normed = half * factors[h * 160 : (h + 1) * 160, k : k + 1] * gain_ref[k : k + 1, :]
            ul[h, :, k * COL : (k + 1) * COL] = normed.astype(BF16)

    def draft_half(half, out):
        def step(i, carry):
            at = pl.ds(pl.multiple_of(i * 256, 256), 256)
            out[:, at] = jnp.dot(ul[half], head_ref[:, at], preferred_element_type=F32)
            return carry

        lax.fori_loop(0, 4, step, 0)

    draft_half(1 - c, cs)
    send(cs, cr, s_c, r_c, core_dev)

    draft_half(c, ds)
    arrived(cr, s_c, r_c, core_dev)
    tops = []
    for k in range(4):
        rows = slice(k * BLK, (k + 1) * BLK)
        part = ds[rows, :] + cr[rows, :]
        ds[rows, :] = part
        tops.append(jnp.maximum(jnp.max(jnp.abs(part), axis=1, keepdims=True), 1e-30))
        code = part * (LEVELS / tops[-1])
        zs[k] = pack(code[:, : LOC // 2], code[:, LOC // 2 :])
    zss[...] = columns_to_rows(tops)
    for k, (other, dev) in enumerate(zh_peers):
        send(zss, zsr.at[zh], s_zs.at[k], r_zs.at[zh], dev)
        send(zs.at[other], zr.at[zh], s_z.at[k], r_z.at[zh], dev)
    zsr[zh] = zss[...]
    own[...] = fold(ds[pl.ds(pl.multiple_of(zh * BLK, 8), BLK), :])
    target = fold(tl_ref[...].astype(F32))

    lane = lax.broadcasted_iota(jnp.int32, (1, 128), 1)
    position = sec * BLK + lane
    sequence = position // SPAN
    offset = position % SPAN
    length = jnp.zeros((1, 128), jnp.int32)
    keep = jnp.zeros((1, 128), jnp.int32)
    for q in range(SEQS):
        length = jnp.where(sequence == q, len_ref[q], length)
        keep = jnp.where(sequence == q, mask_ref[q], keep)
    live = (offset < length) & (lane < BLK)
    weight = jnp.where(live, keep.astype(F32) / (jnp.maximum(length, 1).astype(F32) * SEQS), 0.0)

    wait_all(zh_peers, zsr, s_zs, r_zs)
    steps = rows_to_columns(stack_rows([zsr[other, pl.ds(zh, 1), :] for other, _ in zh_peers])) * (1.0 / LEVELS)
    draft = own[...]
    for k, (other, dev) in enumerate(zh_peers):
        arrived(zr.at[other], s_z.at[k], r_z.at[other], dev)
        draft += jnp.concatenate(unpack(zr[other]), axis=0) * both(steps[:BLK, k : k + 1])

    def per_token(a, op, reduce):
        m = op(op(a[:, :128], a[:, 128:256]), op(a[:, 256:384], a[:, 384:]))
        return reduce(op(m[:BLK], m[BLK:]), axis=1, keepdims=True)

    def top(a):
        return per_token(a, jnp.maximum, jnp.max)

    def add(a):
        return per_token(a, jnp.add, jnp.sum)

    d_top = top(draft)
    d_exp = jnp.exp(draft - both(d_top))
    t_top = top(target)
    t_exp = jnp.exp(target - both(t_top))
    st0[...] = columns_to_rows(
        [d_top, add(d_exp), add(d_exp * draft), t_top, add(t_exp), add(t_exp * (target - draft)), add(t_exp * draft)]
    )
    send_all(xz_peers, lambda other: st0, st1, s_s1, r_s1, j)
    st1[j] = st0[...]
    wait_all(xz_peers, st1, s_s1, r_s1)
    st2[y] = stack_rows(merge_stats([st1[k] for k in range(8)]))
    send_all(y_peers, lambda other: st2.at[y], st2, s_s2, r_s2, y)
    wait_all(y_peers, st2, s_s2, r_s2)
    d_top, d_sum, d_first, t_top, t_sum, cross, t_first = merge_stats([st2[k] for k in range(8)])
    valid = lane < BLK
    d_sum = jnp.where(valid, d_sum, 1.0)
    t_sum = jnp.where(valid, t_sum, 1.0)
    d_lse = d_top + jnp.log(d_sum)
    t_lse = t_top + jnp.log(t_sum)
    loss = weight * (cross / t_sum - t_lse + d_lse)
    scale = LOSS_SCALE * weight
    along = scale * (d_first / d_sum - t_first / t_sum)

    cols = rows_to_columns(stack_rows([d_lse, scale, t_top, scale / t_sum]))
    dlogit = both(cols[:BLK, 1:2]) * jnp.exp(draft - both(cols[:BLK, 0:1])) - both(cols[:BLK, 3:4]) * jnp.exp(
        target - both(cols[:BLK, 2:3])
    )
    dlb[pi] = dlogit.astype(BF16)
    for k, (other, dev) in enumerate(zh_peers):
        send(dlb.at[pi], dlb.at[pi], s_dl.at[k], r_dl.at[pi], dev)
    send(dlb.at[pi], dlb.at[pi], s_fw.at[3], r_dl.at[pi], core_dev)
    qb[pi] = stack_rows([along, loss])
    send_all(sec_peers, lambda other: qb.at[pi], qb, s_q, r_q, pi)
    for k, (other, dev) in enumerate(zh_peers[1:] + zh_peers[:1]):
        slot = c * 4 + other
        arrived(dlb.at[slot], s_dl.at[k], r_dl.at[slot], dev)
        send(dlb.at[slot], dlb.at[slot], s_fw.at[k], r_dl.at[slot], core_dev)

    def grad_half(half):
        for k in range(0, 4, 2):
            pair = [unfold(dlb[half * 4 + k + i].astype(F32)) for i in range(2)]
            dl[half, k * BLK : (k + 2) * BLK] = jnp.concatenate(pair, axis=0).astype(BF16)

        def step(i, carry):
            at = pl.ds(pl.multiple_of(i * 256, 256), 256)
            acc = lax.dot_general(
                dl[half], head_ref[at, :], (((1,), (1,)), ((), ())), preferred_element_type=F32
            )
            rows = pl.ds(pl.multiple_of(half * 160, 16), 160)
            sb2[2 * i, rows] = acc[:, :COL].astype(BF16)
            sb2[2 * i + 1, rows] = acc[:, COL:].astype(BF16)
            return carry

        lax.fori_loop(0, 4, step, 0)

    grad_half(c)
    for zh2 in range(4):
        slot = (1 - c) * 4 + zh2
        arrived(dlb.at[slot], s_fw.at[0], r_dl.at[slot], core_dev)
    grad_half(1 - c)

    vocab_sum(from_bf16, sb2, rb2, a2, b2, p2, dn, s_x2, r_x2, s_y2, r_y2, s_g2, r_g2)

    wait_all(sec_peers, qb, s_q, r_q)
    loss = qb[0, 1:2]
    for k in range(1, 8):
        loss += qb[k, 1:2]
    loss_ref[0, 0] = jnp.sum(loss)
    q_cols = rows_to_columns(stack_rows([qb[k, 0:1] for k in range(8)]))
    gain = gain_ref[pl.ds(j, 1), :]
    gg = jnp.zeros((BLK, COL), F32)
    pair = []
    for k in range(8):
        inv = invc[k]
        joined = jy[k]
        grad = dn[k] * inv
        gg += grad * joined
        pair.append(grad * gain - joined * (q_cols[:BLK, k : k + 1] * inv * inv / WIDTH))
        if k % 2:
            df[j, (k - 1) * BLK : (k + 1) * BLK] = jnp.concatenate(pair, axis=0).astype(BF16)
            pair = []
    send_all(xz_peers, lambda other: df.at[j], df, s_df, r_df, j)
    ggb[j] = jnp.sum(gg, axis=0, keepdims=True)
    send_all(xz_peers, lambda other: ggb.at[j], ggb, s_gg, r_gg, j)
    wait_all(xz_peers, df, s_df, r_df)
    for k in range(8):
        dfl[:, k * COL : (k + 1) * COL] = df[k]

    def out_step(i, carry):
        at = pl.ds(pl.multiple_of(i * 256, 256), 256)
        for k in range(TAPS):
            jg_ref[k * COL : (k + 1) * COL, at] = lax.dot_general(
                tapl[:, k * COL : (k + 1) * COL], dfl[:, at], (((0,), (0,)), ((), ())), preferred_element_type=F32
            )
        return carry

    lax.fori_loop(0, 4, out_step, 0)
    wait_all(xz_peers, ggb, s_gg, r_gg)
    for k in range(8):
        gg_ref[k : k + 1, :] = ggb[k]
    for copy in pending:
        copy.wait_send()


def shards(tap_hidden, join_weight, norm_gain, head_weight, target_logits, seq_lengths, seq_mask):
    vmem = pl.BlockSpec(memory_space=pltpu.VMEM)
    smem = pl.BlockSpec(memory_space=pltpu.SMEM)
    dma = pltpu.SemaphoreType.DMA
    V = pltpu.VMEM
    hbm = pl.BlockSpec(memory_space=pl.ANY)
    scratch = [
        V((TAPS, BLK, COL), BF16), V((TAPS * COL, LOC), BF16), V((8, COL), F32), V((LOC, LOC), BF16),
        V((BLK, LOC), BF16), pltpu.SMEM((SEQS,), jnp.int32), pltpu.SMEM((SEQS,), jnp.int32),
        V((8, 128, COL), BF16), V((TOK, TAPS * COL), BF16),
        V((8, TOK // 2, COL), jnp.int32), V((8, TOK // 2, COL), jnp.int32),
        V((8, BLK, COL), F32), V((8, BLK, COL), F32), V((BLK, COL), F32), V((8, BLK, COL), F32),
        V((8, 1, 384), F32), V((8, TOK // 2, COL), jnp.int32), V((2, TOK // 2, LOC), BF16),
        V((TOK // 2, LOC), F32), V((TOK // 2, LOC), F32), V((TOK // 2, LOC), F32),
        V((2 * BLK, LOC // 2), F32),
        V((4, BLK, LOC // 2), jnp.int32), V((4, BLK, LOC // 2), jnp.int32), V((8, 128), F32), V((4, 8, 128), F32),
        V((8, 1, 384), F32), V((8, BLK, COL), F32),
        V((8, 128), F32), V((8, 8, 128), F32), V((8, 8, 128), F32),
        V((8, 2 * BLK, LOC // 2), BF16), V((2, TOK // 2, LOC), BF16), V((8, 8, 128), F32),
        V((8, TOK, COL), BF16), V((8, TOK, COL), BF16),
        V((8, BLK, COL), F32), V((8, BLK, COL), F32), V((BLK, COL), F32), V((8, BLK, COL), F32),
        V((8, TOK, COL), BF16), V((8, 1, COL), F32), V((TOK, LOC), BF16),
        dma((7,)), dma((3,)), dma((8,)), dma((4,)),
        dma((7,)), dma((8,)), dma((7,)), dma((8,)), dma((7,)), dma((8,)),
        dma((7,)), dma((8,)), dma((7,)), dma((8,)),
        dma, dma,
        dma((3,)), dma((4,)), dma((3,)), dma((4,)),
        dma((7,)), dma((8,)),
        dma((7,)), dma((8,)), dma((7,)), dma((8,)),
        dma((3,)), dma((8,)), dma((4,)),
        dma((7,)), dma((8,)),
        dma((7,)), dma((8,)), dma((7,)), dma((8,)), dma((7,)), dma((8,)),
        dma((7,)), dma((8,)), dma((7,)), dma((8,)),
    ]
    loss, join_grad, gain_grad = pl.pallas_call(
        kernel,
        out_shape=(
            jax.ShapeDtypeStruct((1, 1), F32),
            jax.ShapeDtypeStruct((TAPS * COL, LOC), F32),
            jax.ShapeDtypeStruct((8, COL), F32),
        ),
        in_specs=[hbm] * 7,
        out_specs=(smem, vmem, vmem),
        scratch_shapes=scratch,
        compiler_params=pltpu.CompilerParams(
            collective_id=0, has_side_effects=True, vmem_limit_bytes=60 * 1024 * 1024
        ),
        name="draft_step",
    )(
        tap_hidden,
        join_weight.reshape(TAPS * COL, LOC),
        norm_gain.reshape(8, COL),
        head_weight,
        target_logits,
        seq_lengths,
        seq_mask,
    )
    return loss.reshape(()), join_grad.reshape(TAPS, COL, LOC), gain_grad.reshape(LOC)


def solution(mesh):
    in_specs = (
        P(None, "section", "vocab"),
        P(None, "vocab", "section"),
        P("section"),
        P("section", "vocab"),
        P("section", "vocab"),
        P(),
        P(),
    )
    out_specs = (P(), P(None, "vocab", "section"), P("section"))
    return jax.shard_map(shards, mesh=mesh, in_specs=in_specs, out_specs=out_specs, check_vma=False)
```

```python
import jax
import jax.numpy as jnp
from jax import lax
from jax.experimental import pallas as pl
from jax.experimental.pallas import tpu as pltpu
from jax.sharding import PartitionSpec as P

MESH = pl.DeviceIdType.MESH
F32 = jnp.float32
BF16 = jnp.bfloat16

SPAN = 32
SEQS = 10
LOSS_SCALE = 1024.0
EPS = 1e-05
WIDTH = 8192
TAPS = 3
BLK = 40
SPLITS = (16, 16, 8)
TOK = 320
COL = 128
LOC = 1024


def fold(a):
    return jnp.concatenate([a[:, : LOC // 2], a[:, LOC // 2 :]], axis=0)


def unfold(a):
    rows = a.shape[0] // 2
    return jnp.concatenate([a[:rows], a[rows:]], axis=1)


LEVELS = 32767.0
BOUND = TAPS * COL * 6.0 * 0.0390625


def pack(low, high):
    low = jnp.where(low < 0, low - 0.5, low + 0.5).astype(jnp.int32)
    high = jnp.where(high < 0, high - 0.5, high + 0.5).astype(jnp.int32)
    return (high << 16) | (low & 0xFFFF)


def unpack(word):
    return ((word << 16) >> 16).astype(F32), (word >> 16).astype(F32)


def root_code(a):
    root = jnp.sqrt(jnp.sqrt(jnp.minimum(jnp.abs(a) * (1.0 / BOUND), 1.0))) * LEVELS
    return jnp.where(a < 0, -root, root)


def root_value(code):
    code = code * (1.0 / LEVELS)
    return BOUND * (code * code) * (code * jnp.abs(code))


def both(a):
    return jnp.concatenate([a, a], axis=0)


def columns_to_rows(columns):
    rows = columns[0].shape[0]
    lane = lax.broadcasted_iota(jnp.int32, (rows, 128), 1)
    out = jnp.zeros((rows, 128), F32)
    for i, column in enumerate(columns):
        out = jnp.where(lane == i, column, out)
    out = jnp.concatenate([out, jnp.zeros((128 - rows, 128), F32)], axis=0)
    return out.T[:8]


def stack_rows(rows):
    sub = lax.broadcasted_iota(jnp.int32, (8, 128), 0)
    out = jnp.zeros((8, 128), F32)
    for i, row in enumerate(rows):
        out = jnp.where(sub == i, row, out)
    return out


def rows_to_columns(rows):
    return jnp.concatenate([rows, jnp.zeros((120, 128), F32)], axis=0).T


def merge_stats(parts):
    top_d, top_t = parts[0][0:1], parts[0][3:4]
    for p in parts[1:]:
        top_d = jnp.maximum(top_d, p[0:1])
        top_t = jnp.maximum(top_t, p[3:4])
    sums = [jnp.zeros((1, 128), F32) for _ in range(5)]
    for p in parts:
        a = jnp.exp(p[0:1] - top_d)
        b = jnp.exp(p[3:4] - top_t)
        sums[0] += a * p[1:2]
        sums[1] += a * p[2:3]
        sums[2] += b * p[4:5]
        sums[3] += b * p[5:6]
        sums[4] += b * p[6:7]
    return [top_d, sums[0], sums[1], top_t, sums[2], sums[3], sums[4]]


def chain_scratch(rows):
    V, dma = pltpu.VMEM, pltpu.SemaphoreType.DMA
    i32 = jnp.int32
    padded = -(-8 * rows // 128) * 128
    half = LOC // 2
    buffers = dict(
        tapl=V((8 * rows, TAPS * COL), BF16),
        sb1=V((8, 4 * rows, COL), i32), rb1=V((8, 4 * rows, COL), i32),
        a1=V((8, rows, COL), F32), b1=V((8, rows, COL), F32), p1=V((rows, COL), F32), jy=V((8, rows, COL), F32),
        sqx=V((8, 1, padded), F32), sqb=V((8, 1, padded), F32), invc=V((8, rows, COL), F32),
        ub=V((8, 4 * rows, COL), i32), ul=V((8 * rows, LOC), BF16),
        dd=V((2, 4 * rows, LOC), F32), cr=V((4 * rows, LOC), F32), ds=V((4, rows, LOC), F32),
        zs=V((4, rows, half), i32), zr=V((4, rows, half), i32), zss=V((8, 128), F32), zsr=V((4, 8, 128), F32),
        st0=V((8, 128), F32), st1=V((8, 8, 128), F32), st2=V((8, 8, 128), F32),
        dlb=V((8, 2 * rows, half), BF16), dl=V((8 * rows, LOC), BF16), qb=V((8, 8, 128), F32),
        sb2=V((8, 8 * rows, COL), BF16), rb2=V((8, 8 * rows, COL), BF16),
        a2=V((8, rows, COL), F32), b2=V((8, rows, COL), F32), p2=V((rows, COL), F32), dn=V((8, rows, COL), F32),
        df=V((8, 8 * rows, COL), BF16),
    )
    sems = {}
    for name in ("x1", "y1", "g1", "sx", "u", "sq", "s1", "s2", "q", "x2", "y2", "g2", "df"):
        sems["s_" + name], sems["r_" + name] = dma((7,)), dma((8,))
    for name in ("z", "zs"):
        sems["s_" + name], sems["r_" + name] = dma((3,)), dma((4,))
    sems.update(s_c=dma, r_c=dma, s_dl=dma((3,)), r_dl=dma((8,)), s_fw=dma((4,)))
    return buffers | sems


def shared_scratch():
    V, dma = pltpu.VMEM, pltpu.SemaphoreType.DMA
    return dict(
        tap=V((TAPS, BLK, COL), BF16), jw=V((TAPS * COL, LOC), BF16), gain=V((8, COL), F32),
        head=V((LOC, LOC), BF16), tl=V((BLK, LOC), BF16),
        len=pltpu.SMEM((SEQS,), jnp.int32), mask=pltpu.SMEM((SEQS,), jnp.int32),
        tapg=V((8, 128, COL), BF16), ggb=V((8, 1, COL), F32),
        s_in=dma((7,)), s_tap=dma((3,)), r_tap=dma((8,)), s_tf=dma((4,)), s_gg=dma((7,)), r_gg=dma((8,)),
    )


class Names:
    def __init__(self, names, refs):
        self.__dict__.update(zip(names, refs, strict=True))


def kernel(
    tap_hbm, jw_hbm, gain_hbm, head_hbm, tl_hbm, len_hbm, mask_hbm, loss_ref, gg_ref, taps_ref, grads_ref, *scratch
):
    names = list(shared_scratch())
    m, scratch = Names(names, scratch[: len(names)]), scratch[len(names) :]
    chains = []
    for rows in SPLITS:
        names = list(chain_scratch(rows))
        chains.append(Names(names, scratch[: len(names)]))
        scratch = scratch[len(names) :]

    sec = lax.axis_index("section")
    voc = lax.axis_index("vocab")
    zh, c = lax.div(sec, 2), lax.rem(sec, 2)
    zl, y, x = lax.div(voc, 32), lax.rem(lax.div(voc, 4), 8), lax.rem(voc, 4)
    j = zl * 4 + x
    pi = c * 4 + zh

    sec_peers = []
    for a, b in ((2, 0), (2, 1), (1, 0), (3, 0), (1, 1), (3, 1), (0, 1)):
        zh2, c2 = lax.rem(zh + a, 4), lax.rem(c + b, 2)
        sec_peers.append((c2 * 4 + zh2, (zh2 * 2 + c2, voc)))
    zh_peers = []
    for a in (2, 1, 3):
        zh2 = lax.rem(zh + a, 4)
        zh_peers.append((zh2, (zh2 * 2 + c, voc)))
    near_first = zh_peers[1:] + zh_peers[:1]
    core_dev = (zh * 2 + (1 - c), voc)
    xz_peers = []
    for a, b in ((1, 2), (1, 1), (1, 3), (0, 2), (0, 1), (0, 3), (1, 0)):
        zl2, x2 = lax.rem(zl + a, 2), lax.rem(x + b, 4)
        xz_peers.append((zl2 * 4 + x2, (sec, zl2 * 32 + y * 4 + x2)))
    y_peers = []
    for a in (4, 3, 5, 2, 6, 1, 7):
        y2 = lax.rem(y + a, 8)
        y_peers.append((y2, (sec, zl * 32 + y2 * 4 + x)))

    inputs = (
        (tap_hbm, m.tap), (jw_hbm, m.jw), (gain_hbm, m.gain), (len_hbm, m.len), (mask_hbm, m.mask),
        (head_hbm, m.head), (tl_hbm, m.tl),
    )
    loads = [pltpu.make_async_copy(src, dst, m.s_in.at[i]) for i, (src, dst) in enumerate(inputs)]
    for load in loads:
        load.start()

    barrier = pltpu.get_barrier_semaphore()
    for _, dev in sec_peers + xz_peers + y_peers:
        pl.semaphore_signal(barrier, inc=1, device_id=dev, device_id_type=MESH)
    loads[0].wait()
    taps = [m.tap[k].astype(F32) for k in range(TAPS)] + [jnp.zeros((128 - TAPS * BLK, COL), F32)]
    m.tapg[pi] = jnp.concatenate(taps, axis=0).astype(BF16)
    pl.semaphore_wait(barrier, 21)

    pending = []

    def send(src, dst, s_sem, r_sem, dev):
        copy = pltpu.make_async_remote_copy(src, dst, s_sem, r_sem, device_id=dev, device_id_type=MESH)
        copy.start()
        pending.append(copy)

    def send_all(peers, src, dst, s_sem, r_sem, slot):
        for k, (other, dev) in enumerate(peers):
            send(src(other), dst.at[slot], s_sem.at[k], r_sem.at[slot], dev)

    def arrived(dst, s_sem, r_sem, dev):
        pltpu.make_async_remote_copy(dst, dst, s_sem, r_sem, device_id=dev, device_id_type=MESH).wait_recv()

    def wait_all(peers, dst, s_sem, r_sem):
        for k, (other, dev) in enumerate(peers):
            arrived(dst.at[other], s_sem.at[k], r_sem.at[other], dev)

    for k, (other, dev) in enumerate(zh_peers):
        send(m.tapg.at[pi], m.tapg.at[pi], m.s_tap.at[k], m.r_tap.at[pi], dev)
    send(m.tapg.at[pi], m.tapg.at[pi], m.s_tf.at[3], m.r_tap.at[pi], core_dev)
    for k, (other, dev) in enumerate(near_first):
        slot = c * 4 + other
        arrived(m.tapg.at[slot], m.s_tap.at[k], m.r_tap.at[slot], dev)
        send(m.tapg.at[slot], m.tapg.at[slot], m.s_tf.at[k], m.r_tap.at[slot], core_dev)
    for load in loads[1:]:
        load.wait()
    for zh2 in range(4):
        slot = (1 - c) * 4 + zh2
        arrived(m.tapg.at[slot], m.s_tf.at[0], m.r_tap.at[slot], core_dev)

    def from_roots(rb):
        low, high = [root_value(half) for half in unpack(rb[0])]
        for k in range(1, 8):
            more = [root_value(half) for half in unpack(rb[k])]
            low, high = low + more[0], high + more[1]
        return jnp.concatenate([low, high], axis=0)

    def from_bf16(rb):
        total = rb[0].astype(F32)
        for k in range(1, 8):
            total += rb[k].astype(F32)
        return total

    def vocab_sum(collect, rows, sb, rb, a_buf, b_buf, p_buf, out, s_x, r_x, s_y, r_y, s_g, r_g):
        send_all(xz_peers, lambda other: sb.at[other], rb, s_x, r_x, j)
        rb[j] = sb[j]
        yield
        wait_all(xz_peers, rb, s_x, r_x)
        total = collect(rb)
        for k in range(8):
            a_buf[k] = total[k * rows : (k + 1) * rows]
        send_all(y_peers, lambda other: a_buf.at[other], b_buf, s_y, r_y, y)
        b_buf[y] = a_buf[y]
        yield
        wait_all(y_peers, b_buf, s_y, r_y)
        piece = b_buf[0]
        for k in range(1, 8):
            piece += b_buf[k]
        p_buf[...] = piece
        send_all(y_peers, lambda other: p_buf, out, s_g, r_g, y)
        out[y] = piece
        yield
        wait_all(y_peers, out, s_g, r_g)

    results = []

    def chain(index):
        w = chains[index]
        rows, first = SPLITS[index], sum(SPLITS[:index])
        half, tokens = 4 * rows, 8 * rows
        padded = -(-tokens // 128) * 128

        blocks = [m.tapg[p].astype(F32) for p in range(8)]
        for k in range(TAPS):
            at = k * BLK + first
            tap = jnp.concatenate([b[at : at + rows] for b in blocks], axis=0)
            w.tapl[:, k * COL : (k + 1) * COL] = tap.astype(BF16)
        taps_ref[8 * first : 8 * first + tokens, :] = w.tapl[...]

        def join_step(i, carry):
            at = pl.ds(pl.multiple_of(i * 256, 256), 256)
            acc = root_code(jnp.dot(w.tapl[...], m.jw[:, at], preferred_element_type=F32))
            w.sb1[2 * i] = pack(acc[:half, :COL], acc[half:, :COL])
            w.sb1[2 * i + 1] = pack(acc[:half, COL:], acc[half:, COL:])
            return carry

        lax.fori_loop(0, 4, join_step, 0)
        yield from vocab_sum(
            from_roots, rows, w.sb1, w.rb1, w.a1, w.b1, w.p1, w.jy, w.s_x1, w.r_x1, w.s_y1, w.r_y1, w.s_g1, w.r_g1
        )

        joined = jnp.concatenate([w.jy[k] for k in range(8)], axis=0)
        square = joined * joined
        tall = square
        if padded > tokens:
            tall = jnp.concatenate([square, jnp.zeros((padded - tokens, COL), F32)], axis=0)
        w.sqx[j] = jnp.sum(tall.T, axis=0, keepdims=True)
        send_all(xz_peers, lambda other: w.sqx.at[j], w.sqx, w.s_sx, w.r_sx, j)
        code = joined * (LEVELS * lax.rsqrt(jnp.maximum(jnp.sum(square, axis=1, keepdims=True), 1e-30)))
        w.ub[j] = pack(code[:half], code[half:])
        send_all(xz_peers, lambda other: w.ub.at[j], w.ub, w.s_u, w.r_u, j)
        yield
        wait_all(xz_peers, w.sqx, w.s_sx, w.r_sx)
        square = w.sqx[0]
        for k in range(1, 8):
            square += w.sqx[k]
        w.sqb[pi] = square
        send_all(sec_peers, lambda other: w.sqb.at[pi], w.sqb, w.s_sq, w.r_sq, pi)
        yield
        wait_all(sec_peers, w.sqb, w.s_sq, w.r_sq)
        square = w.sqb[0]
        for k in range(1, 8):
            square += w.sqb[k]
        inverse = lax.rsqrt(square / WIDTH + EPS)
        factors = [jnp.sqrt(w.sqx[k]) * (1.0 / LEVELS) * inverse for k in range(8)]
        factors = jnp.concatenate(factors + [jnp.zeros((120, padded), F32)], axis=0).T
        inverse = jnp.broadcast_to(inverse, (128, padded)).T
        for k in range(8):
            w.invc[k] = inverse[k * rows : (k + 1) * rows]
        wait_all(xz_peers, w.ub, w.s_u, w.r_u)
        for k in range(8):
            for h, part in enumerate(unpack(w.ub[k])):
                normed = part * factors[h * half : (h + 1) * half, k : k + 1] * m.gain[k : k + 1, :]
                w.ul[h * half : (h + 1) * half, k * COL : (k + 1) * COL] = normed.astype(BF16)

        def draft_step(i, carry):
            at = pl.ds(pl.multiple_of(i * 256, 256), 256)
            acc = jnp.dot(w.ul[...], m.head[:, at], preferred_element_type=F32)
            w.dd[0, :, at] = acc[:half]
            w.dd[1, :, at] = acc[half:]
            return carry

        lax.fori_loop(0, 4, draft_step, 0)
        send(w.dd.at[1 - c], w.cr, w.s_c, w.r_c, core_dev)

        lane = lax.broadcasted_iota(jnp.int32, (1, 128), 1)
        valid = lane < rows
        position = sec * BLK + first + lane
        sequence = position // SPAN
        offset = position % SPAN
        length = jnp.zeros((1, 128), jnp.int32)
        keep = jnp.zeros((1, 128), jnp.int32)
        for q in range(SEQS):
            length = jnp.where(sequence == q, m.len[q], length)
            keep = jnp.where(sequence == q, m.mask[q], keep)
        live = (offset < length) & valid
        weight = jnp.where(live, keep.astype(F32) / (jnp.maximum(length, 1).astype(F32) * SEQS), 0.0)
        arrived(w.cr, w.s_c, w.r_c, core_dev)
        tops = []
        for k in range(4):
            at = slice(k * rows, (k + 1) * rows)
            part = w.dd[c, at, :] + w.cr[at, :]
            w.ds[k] = part
            tops.append(jnp.maximum(jnp.max(jnp.abs(part), axis=1, keepdims=True), 1e-30))
            code = part * (LEVELS / tops[-1])
            w.zs[k] = pack(code[:, : LOC // 2], code[:, LOC // 2 :])
        w.zss[...] = columns_to_rows(tops)
        for k, (other, dev) in enumerate(zh_peers):
            send(w.zss, w.zsr.at[zh], w.s_zs.at[k], w.r_zs.at[zh], dev)
            send(w.zs.at[other], w.zr.at[zh], w.s_z.at[k], w.r_z.at[zh], dev)
        draft = fold(w.ds[zh])
        target = fold(m.tl[...].astype(F32)[first : first + rows])
        yield
        wait_all(zh_peers, w.zsr, w.s_zs, w.r_zs)
        steps = rows_to_columns(stack_rows([w.zsr[other, pl.ds(zh, 1), :] for other, _ in zh_peers])) * (1.0 / LEVELS)
        for k, (other, dev) in enumerate(zh_peers):
            arrived(w.zr.at[other], w.s_z.at[k], w.r_z.at[other], dev)
            draft += jnp.concatenate(unpack(w.zr[other]), axis=0) * both(steps[:rows, k : k + 1])

        def per_token(a, op, reduce):
            a = op(op(a[:, :128], a[:, 128:256]), op(a[:, 256:384], a[:, 384:]))
            return reduce(op(a[:rows], a[rows:]), axis=1, keepdims=True)

        def top(a):
            return per_token(a, jnp.maximum, jnp.max)

        def add(a):
            return per_token(a, jnp.add, jnp.sum)

        d_top = top(draft)
        d_exp = jnp.exp(draft - both(d_top))
        t_top = top(target)
        t_exp = jnp.exp(target - both(t_top))
        w.st0[...] = columns_to_rows(
            [d_top, add(d_exp), add(d_exp * draft), t_top, add(t_exp), add(t_exp * (target - draft)), add(t_exp * draft)]
        )
        send_all(xz_peers, lambda other: w.st0, w.st1, w.s_s1, w.r_s1, j)
        w.st1[j] = w.st0[...]
        yield
        wait_all(xz_peers, w.st1, w.s_s1, w.r_s1)
        w.st2[y] = stack_rows(merge_stats([w.st1[k] for k in range(8)]))
        send_all(y_peers, lambda other: w.st2.at[y], w.st2, w.s_s2, w.r_s2, y)
        yield
        wait_all(y_peers, w.st2, w.s_s2, w.r_s2)
        d_top, d_sum, d_first, t_top, t_sum, cross, t_first = merge_stats([w.st2[k] for k in range(8)])
        d_sum = jnp.where(valid, d_sum, 1.0)
        t_sum = jnp.where(valid, t_sum, 1.0)
        d_lse = d_top + jnp.log(d_sum)
        t_lse = t_top + jnp.log(t_sum)
        loss = weight * (cross / t_sum - t_lse + d_lse)
        scale = LOSS_SCALE * weight
        along = scale * (d_first / d_sum - t_first / t_sum)
        cols = rows_to_columns(stack_rows([d_lse, scale, t_top, scale / t_sum]))[:rows]
        dlogit = both(cols[:, 1:2]) * jnp.exp(draft - both(cols[:, 0:1]))
        dlogit -= both(cols[:, 3:4]) * jnp.exp(target - both(cols[:, 2:3]))
        w.dlb[pi] = dlogit.astype(BF16)
        for k, (other, dev) in enumerate(zh_peers):
            send(w.dlb.at[pi], w.dlb.at[pi], w.s_dl.at[k], w.r_dl.at[pi], dev)
        send(w.dlb.at[pi], w.dlb.at[pi], w.s_fw.at[3], w.r_dl.at[pi], core_dev)
        w.qb[pi] = stack_rows([along, loss])
        send_all(sec_peers, lambda other: w.qb.at[pi], w.qb, w.s_q, w.r_q, pi)
        yield
        for k, (other, dev) in enumerate(near_first):
            slot = c * 4 + other
            arrived(w.dlb.at[slot], w.s_dl.at[k], w.r_dl.at[slot], dev)
            send(w.dlb.at[slot], w.dlb.at[slot], w.s_fw.at[k], w.r_dl.at[slot], core_dev)
        for zh2 in range(4):
            slot = (1 - c) * 4 + zh2
            arrived(w.dlb.at[slot], w.s_fw.at[0], w.r_dl.at[slot], core_dev)
        for k in range(0, 8, 2):
            pair = [unfold(w.dlb[k + i].astype(F32)) for i in range(2)]
            w.dl[k * rows : (k + 2) * rows] = jnp.concatenate(pair, axis=0).astype(BF16)

        def grad_step(i, carry):
            at = pl.ds(pl.multiple_of(i * 256, 256), 256)
            acc = lax.dot_general(w.dl[...], m.head[at, :], (((1,), (1,)), ((), ())), preferred_element_type=F32)
            w.sb2[2 * i] = acc[:, :COL].astype(BF16)
            w.sb2[2 * i + 1] = acc[:, COL:].astype(BF16)
            return carry

        lax.fori_loop(0, 4, grad_step, 0)
        yield from vocab_sum(
            from_bf16, rows, w.sb2, w.rb2, w.a2, w.b2, w.p2, w.dn, w.s_x2, w.r_x2, w.s_y2, w.r_y2, w.s_g2, w.r_g2
        )

        wait_all(sec_peers, w.qb, w.s_q, w.r_q)
        loss = w.qb[0, 1:2]
        for k in range(1, 8):
            loss += w.qb[k, 1:2]
        q_cols = rows_to_columns(stack_rows([w.qb[k, 0:1] for k in range(8)]))[:rows]
        gain = m.gain[pl.ds(j, 1), :]
        gg = jnp.zeros((rows, COL), F32)
        pair = []
        for k in range(8):
            inv = w.invc[k]
            joined = w.jy[k]
            grad = w.dn[k] * inv
            gg += grad * joined
            pair.append(grad * gain - joined * (q_cols[:, k : k + 1] * inv * inv / WIDTH))
            if k % 2:
                w.df[j, (k - 1) * rows : (k + 1) * rows] = jnp.concatenate(pair, axis=0).astype(BF16)
                pair = []
        send_all(xz_peers, lambda other: w.df.at[j], w.df, w.s_df, w.r_df, j)
        results.append((loss, jnp.sum(gg, axis=0, keepdims=True)))
        if index == len(SPLITS) - 1:
            m.ggb[j] = sum(gg for _, gg in results)
            send_all(xz_peers, lambda other: m.ggb.at[j], m.ggb, m.s_gg, m.r_gg, j)
            loss_ref[0, 0] = jnp.sum(sum(loss for loss, _ in results))
        yield
        wait_all(xz_peers, w.df, w.s_df, w.r_df)
        for k in range(8):
            grads_ref[8 * first : 8 * first + tokens, k * COL : (k + 1) * COL] = w.df[k]

    running = [chain(i) for i in range(len(SPLITS))]
    while running:
        running = [one for one in running if next(one, running) is not running]
    wait_all(xz_peers, m.ggb, m.s_gg, m.r_gg)
    for k in range(8):
        gg_ref[k : k + 1, :] = m.ggb[k]
    for copy in pending:
        copy.wait_send()


def last_kernel(taps_ref, grads_ref, gg_in, loss_in, out_ref, gg_ref, loss_ref):
    out_ref[...] = lax.dot_general(
        taps_ref[...], grads_ref[...], (((0,), (0,)), ((), ())), preferred_element_type=F32
    )
    gg_ref[...] = gg_in[...]
    loss_ref[0, 0] = loss_in[0, 0]


def shards(tap_hidden, join_weight, norm_gain, head_weight, target_logits, seq_lengths, seq_mask):
    vmem = pl.BlockSpec(memory_space=pltpu.VMEM)
    smem = pl.BlockSpec(memory_space=pltpu.SMEM)
    hbm = pl.BlockSpec(memory_space=pl.ANY)
    scratch = list(shared_scratch().values())
    for rows in SPLITS:
        scratch += list(chain_scratch(rows).values())
    loss, gain_grad, taps, grads = pl.pallas_call(
        kernel,
        out_shape=(
            jax.ShapeDtypeStruct((1, 1), F32),
            jax.ShapeDtypeStruct((8, COL), F32),
            jax.ShapeDtypeStruct((TOK, TAPS * COL), BF16),
            jax.ShapeDtypeStruct((TOK, LOC), BF16),
        ),
        in_specs=[hbm] * 7,
        out_specs=(smem, vmem, vmem, vmem),
        scratch_shapes=scratch,
        compiler_params=pltpu.CompilerParams(
            collective_id=0, has_side_effects=True, vmem_limit_bytes=60 * 1024 * 1024
        ),
        name="draft_step",
    )(
        tap_hidden,
        join_weight.reshape(TAPS * COL, LOC),
        norm_gain.reshape(8, COL),
        head_weight,
        target_logits,
        seq_lengths,
        seq_mask,
    )
    tile = 256
    join_grad, gain_grad, loss = pl.pallas_call(
        last_kernel,
        grid=(LOC // tile,),
        out_shape=(
            jax.ShapeDtypeStruct((TAPS * COL, LOC), F32),
            jax.ShapeDtypeStruct((8, COL), F32),
            jax.ShapeDtypeStruct((1, 1), F32),
        ),
        in_specs=[
            pl.BlockSpec((TOK, TAPS * COL), lambda i: (0, 0)),
            pl.BlockSpec((TOK, tile), lambda i: (0, i)),
            pl.BlockSpec((8, COL), lambda i: (0, 0)),
            smem,
        ],
        out_specs=(
            pl.BlockSpec((TAPS * COL, tile), lambda i: (0, i)),
            pl.BlockSpec((8, COL), lambda i: (0, 0)),
            smem,
        ),
        compiler_params=pltpu.CompilerParams(vmem_limit_bytes=60 * 1024 * 1024),
        name="join_gradient",
    )(taps, grads, gain_grad, loss)
    return loss.reshape(()), join_grad.reshape(TAPS, COL, LOC), gain_grad.reshape(LOC)


def solution(mesh):
    in_specs = (
        P(None, "section", "vocab"),
        P(None, "vocab", "section"),
        P("section"),
        P("section", "vocab"),
        P("section", "vocab"),
        P(),
        P(),
    )
    out_specs = (P(), P(None, "vocab", "section"), P("section"))
    return jax.shard_map(shards, mesh=mesh, in_specs=in_specs, out_specs=out_specs, check_vma=False)
```

```python
import jax
import jax.numpy as jnp
from jax import lax
from jax.experimental import pallas as pl
from jax.experimental.pallas import tpu as pltpu
from jax.sharding import PartitionSpec as P

MESH = pl.DeviceIdType.MESH
F32 = jnp.float32
BF16 = jnp.bfloat16

SPAN = 32
SEQS = 10
LOSS_SCALE = 1024.0
EPS = 1e-05
WIDTH = 8192
TAPS = 3
BLK = 40
SPLITS = (16, 16, 8)
TOK = 320
COL = 128
LOC = 1024


def fold(a):
    return jnp.concatenate([a[:, : LOC // 2], a[:, LOC // 2 :]], axis=0)


def unfold(a):
    rows = a.shape[0] // 2
    return jnp.concatenate([a[:rows], a[rows:]], axis=1)


LEVELS = 32767.0
BOUND = TAPS * COL * 6.0 * 0.0390625


def pack(low, high):
    low = jnp.where(low < 0, low - 0.5, low + 0.5).astype(jnp.int32)
    high = jnp.where(high < 0, high - 0.5, high + 0.5).astype(jnp.int32)
    return (high << 16) | (low & 0xFFFF)


def unpack(word):
    return ((word << 16) >> 16).astype(F32), (word >> 16).astype(F32)


def root_code(a):
    root = jnp.sqrt(jnp.sqrt(jnp.minimum(jnp.abs(a) * (1.0 / BOUND), 1.0))) * LEVELS
    return jnp.where(a < 0, -root, root)


def root_value(code):
    code = code * (1.0 / LEVELS)
    return BOUND * (code * code) * (code * jnp.abs(code))


def both(a):
    return jnp.concatenate([a, a], axis=0)


def columns_to_rows(columns):
    rows = columns[0].shape[0]
    lane = lax.broadcasted_iota(jnp.int32, (rows, 128), 1)
    out = jnp.zeros((rows, 128), F32)
    for i, column in enumerate(columns):
        out = jnp.where(lane == i, column, out)
    out = jnp.concatenate([out, jnp.zeros((128 - rows, 128), F32)], axis=0)
    return out.T[:8]


def stack_rows(rows):
    sub = lax.broadcasted_iota(jnp.int32, (8, 128), 0)
    out = jnp.zeros((8, 128), F32)
    for i, row in enumerate(rows):
        out = jnp.where(sub == i, row, out)
    return out


def rows_to_columns(rows):
    return jnp.concatenate([rows, jnp.zeros((120, 128), F32)], axis=0).T


def merge_stats(parts):
    top_d, top_t = parts[0][0:1], parts[0][3:4]
    for p in parts[1:]:
        top_d = jnp.maximum(top_d, p[0:1])
        top_t = jnp.maximum(top_t, p[3:4])
    sums = [jnp.zeros((1, 128), F32) for _ in range(5)]
    for p in parts:
        a = jnp.exp(p[0:1] - top_d)
        b = jnp.exp(p[3:4] - top_t)
        sums[0] += a * p[1:2]
        sums[1] += a * p[2:3]
        sums[2] += b * p[4:5]
        sums[3] += b * p[5:6]
        sums[4] += b * p[6:7]
    return [top_d, sums[0], sums[1], top_t, sums[2], sums[3], sums[4]]


def chain_scratch(rows):
    V, dma = pltpu.VMEM, pltpu.SemaphoreType.DMA
    i32 = jnp.int32
    padded = -(-8 * rows // 128) * 128
    half = LOC // 2
    buffers = dict(
        tapl=V((8 * rows, TAPS * COL), BF16),
        sb1=V((8, 4 * rows, COL), i32), rb1=V((8, 4 * rows, COL), i32),
        a1=V((8, rows, COL), F32), b1=V((8, rows, COL), F32), p1=V((rows, COL), F32), jy=V((8, rows, COL), F32),
        sqx=V((8, 1, padded), F32), sqb=V((8, 1, padded), F32), invc=V((8, rows, COL), F32),
        ub=V((8, 4 * rows, COL), i32), ul=V((8 * rows, LOC), BF16),
        dd=V((2, 4 * rows, LOC), F32), cr=V((4 * rows, LOC), F32), ds=V((4, rows, LOC), F32),
        zs=V((4, rows, half), i32), zr=V((4, rows, half), i32), zss=V((8, 128), F32), zsr=V((4, 8, 128), F32),
        st0=V((8, 128), F32), st1=V((8, 8, 128), F32), st2=V((8, 8, 128), F32),
        dlb=V((8, 2 * rows, half), BF16), dl=V((8 * rows, LOC), BF16), qb=V((8, 8, 128), F32),
        sb2=V((8, 8 * rows, COL), BF16), rb2=V((8, 8 * rows, COL), BF16),
        a2=V((8, rows, COL), F32), b2=V((8, rows, COL), F32), p2=V((rows, COL), F32), dn=V((8, rows, COL), F32),
        df=V((8, 8 * rows, COL), BF16),
    )
    names = ("x1", "y1", "g1", "sx", "u", "sq", "s1", "s2", "q", "x2", "y2", "g2", "df", "z", "zs", "c", "fw")
    sems = {side + name: dma for name in names for side in ("s_", "r_")}
    sems.update(s_dl=dma, r_dl=dma((4,)))
    return buffers | sems


def shared_scratch():
    V, dma = pltpu.VMEM, pltpu.SemaphoreType.DMA
    return dict(
        tap=V((TAPS, BLK, COL), BF16), jw=V((TAPS * COL, LOC), BF16), gain=V((8, COL), F32),
        head=V((LOC, LOC), BF16), tl=V((BLK, LOC), BF16),
        len=pltpu.SMEM((SEQS,), jnp.int32), mask=pltpu.SMEM((SEQS,), jnp.int32),
        tapg=V((8, 128, COL), BF16), ggb=V((8, 1, COL), F32),
        s_in=dma((7,)), s_tap=dma, r_tap=dma((4,)), s_tf=dma, r_tf=dma, s_gg=dma, r_gg=dma,
    )


class Names:
    def __init__(self, names, refs):
        self.__dict__.update(zip(names, refs, strict=True))


def kernel(
    tap_hbm, jw_hbm, gain_hbm, head_hbm, tl_hbm, len_hbm, mask_hbm, loss_ref, gg_ref, taps_ref, grads_ref, *scratch
):
    names = list(shared_scratch())
    m, scratch = Names(names, scratch[: len(names)]), scratch[len(names) :]
    chains = []
    for rows in SPLITS:
        names = list(chain_scratch(rows))
        chains.append(Names(names, scratch[: len(names)]))
        scratch = scratch[len(names) :]

    sec = lax.axis_index("section")
    voc = lax.axis_index("vocab")
    zh, c = lax.div(sec, 2), lax.rem(sec, 2)
    zl, y, x = lax.div(voc, 32), lax.rem(lax.div(voc, 4), 8), lax.rem(voc, 4)
    j = zl * 4 + x
    pi = c * 4 + zh

    sec_peers = []
    for a, b in ((2, 0), (2, 1), (1, 0), (3, 0), (1, 1), (3, 1), (0, 1)):
        zh2, c2 = lax.rem(zh + a, 4), lax.rem(c + b, 2)
        sec_peers.append((c2 * 4 + zh2, (zh2 * 2 + c2, voc)))
    zh_peers = []
    for a in (2, 1, 3):
        zh2 = lax.rem(zh + a, 4)
        zh_peers.append((zh2, (zh2 * 2 + c, voc)))
    near_first = zh_peers[1:] + zh_peers[:1]
    core_dev = (zh * 2 + (1 - c), voc)
    xz_peers = []
    for a, b in ((1, 2), (1, 1), (1, 3), (0, 2), (0, 1), (0, 3), (1, 0)):
        zl2, x2 = lax.rem(zl + a, 2), lax.rem(x + b, 4)
        xz_peers.append((zl2 * 4 + x2, (sec, zl2 * 32 + y * 4 + x2)))
    y_peers = []
    for a in (4, 3, 5, 2, 6, 1, 7):
        y2 = lax.rem(y + a, 8)
        y_peers.append((y2, (sec, zl * 32 + y2 * 4 + x)))

    inputs = (
        (tap_hbm, m.tap), (jw_hbm, m.jw), (gain_hbm, m.gain), (len_hbm, m.len), (mask_hbm, m.mask),
        (head_hbm, m.head), (tl_hbm, m.tl),
    )
    loads = [pltpu.make_async_copy(src, dst, m.s_in.at[i]) for i, (src, dst) in enumerate(inputs)]
    for load in loads:
        load.start()

    barrier = pltpu.get_barrier_semaphore()
    for _, dev in sec_peers + xz_peers + y_peers:
        pl.semaphore_signal(barrier, inc=1, device_id=dev, device_id_type=MESH)
    loads[0].wait()
    taps = [m.tap[k].astype(F32) for k in range(TAPS)] + [jnp.zeros((128 - TAPS * BLK, COL), F32)]
    m.tapg[pi] = jnp.concatenate(taps, axis=0).astype(BF16)
    pl.semaphore_wait(barrier, 21)

    def copy_to(src, dst, s_sem, r_sem, dev):
        return pltpu.make_async_remote_copy(src, dst, s_sem, r_sem, device_id=dev, device_id_type=MESH)

    sent = []

    def send_all(peers, src, dst, s_sem, r_sem, slot):
        for other, dev in peers:
            copy_to(src(other), dst.at[slot], s_sem, r_sem, dev).start()
        whole = dst.at[pl.ds(0, len(peers))]
        sent.append(copy_to(whole, whole, s_sem, r_sem, peers[0][1]))

    def settle(first):
        for copy in sent[:first]:
            copy.wait_send()
        del sent[:first]

    def wait_all(peers, dst, s_sem, r_sem):
        whole = dst.at[pl.ds(0, len(peers))]
        copy_to(whole, whole, s_sem, r_sem, peers[0][1]).wait_recv()

    def spread(buf, s_near, r_near, s_core, r_core):
        for other, dev in zh_peers:
            copy_to(buf.at[pi], buf.at[pi], s_near, r_near.at[zh], dev).start()
        copy_to(buf.at[pi], buf.at[pi], s_core, r_core, core_dev).start()

    def relay(buf, s_near, r_near, s_core, r_core):
        for other, dev in near_first:
            slot = c * 4 + other
            copy_to(buf.at[slot], buf.at[slot], s_near, r_near.at[other], dev).wait_recv()
            copy_to(buf.at[slot], buf.at[slot], s_core, r_core, core_dev).start()
        three, four = buf.at[pl.ds(0, 3)], buf.at[pl.ds(0, 4)]
        copy_to(three, three, s_near, r_near.at[0], core_dev).wait_send()
        last = copy_to(four, four, s_core, r_core, core_dev)
        last.wait_recv()
        sent.append(last)

    spread(m.tapg, m.s_tap, m.r_tap, m.s_tf, m.r_tf)
    for load in loads[1:]:
        load.wait()
    relay(m.tapg, m.s_tap, m.r_tap, m.s_tf, m.r_tf)

    def from_roots(rb):
        low, high = [root_value(half) for half in unpack(rb[0])]
        for k in range(1, 8):
            more = [root_value(half) for half in unpack(rb[k])]
            low, high = low + more[0], high + more[1]
        return jnp.concatenate([low, high], axis=0)

    def from_bf16(rb):
        total = rb[0].astype(F32)
        for k in range(1, 8):
            total += rb[k].astype(F32)
        return total

    def vocab_sum(collect, rows, sb, rb, a_buf, b_buf, p_buf, out, s_x, r_x, s_y, r_y, s_g, r_g):
        send_all(xz_peers, lambda other: sb.at[other], rb, s_x, r_x, j)
        rb[j] = sb[j]
        yield
        wait_all(xz_peers, rb, s_x, r_x)
        total = collect(rb)
        for k in range(8):
            a_buf[k] = total[k * rows : (k + 1) * rows]
        send_all(y_peers, lambda other: a_buf.at[other], b_buf, s_y, r_y, y)
        b_buf[y] = a_buf[y]
        yield
        wait_all(y_peers, b_buf, s_y, r_y)
        piece = b_buf[0]
        for k in range(1, 8):
            piece += b_buf[k]
        p_buf[...] = piece
        send_all(y_peers, lambda other: p_buf, out, s_g, r_g, y)
        out[y] = piece
        yield
        wait_all(y_peers, out, s_g, r_g)

    results = []

    def chain(index):
        w = chains[index]
        rows, first = SPLITS[index], sum(SPLITS[:index])
        half, tokens = 4 * rows, 8 * rows
        padded = -(-tokens // 128) * 128

        blocks = [m.tapg[p].astype(F32) for p in range(8)]
        for k in range(TAPS):
            at = k * BLK + first
            tap = jnp.concatenate([b[at : at + rows] for b in blocks], axis=0)
            w.tapl[:, k * COL : (k + 1) * COL] = tap.astype(BF16)
        taps_ref[8 * first : 8 * first + tokens, :] = w.tapl[...]

        def join_step(i, carry):
            at = pl.ds(pl.multiple_of(i * 256, 256), 256)
            acc = root_code(jnp.dot(w.tapl[...], m.jw[:, at], preferred_element_type=F32))
            w.sb1[2 * i] = pack(acc[:half, :COL], acc[half:, :COL])
            w.sb1[2 * i + 1] = pack(acc[:half, COL:], acc[half:, COL:])
            return carry

        lax.fori_loop(0, 4, join_step, 0)
        yield from vocab_sum(
            from_roots, rows, w.sb1, w.rb1, w.a1, w.b1, w.p1, w.jy, w.s_x1, w.r_x1, w.s_y1, w.r_y1, w.s_g1, w.r_g1
        )

        joined = jnp.concatenate([w.jy[k] for k in range(8)], axis=0)
        square = joined * joined
        tall = square
        if padded > tokens:
            tall = jnp.concatenate([square, jnp.zeros((padded - tokens, COL), F32)], axis=0)
        w.sqx[j] = jnp.sum(tall.T, axis=0, keepdims=True)
        send_all(xz_peers, lambda other: w.sqx.at[j], w.sqx, w.s_sx, w.r_sx, j)
        code = joined * (LEVELS * lax.rsqrt(jnp.maximum(jnp.sum(square, axis=1, keepdims=True), 1e-30)))
        w.ub[j] = pack(code[:half], code[half:])
        send_all(xz_peers, lambda other: w.ub.at[j], w.ub, w.s_u, w.r_u, j)
        yield
        wait_all(xz_peers, w.sqx, w.s_sx, w.r_sx)
        square = w.sqx[0]
        for k in range(1, 8):
            square += w.sqx[k]
        w.sqb[pi] = square
        send_all(sec_peers, lambda other: w.sqb.at[pi], w.sqb, w.s_sq, w.r_sq, pi)
        yield
        wait_all(sec_peers, w.sqb, w.s_sq, w.r_sq)
        square = w.sqb[0]
        for k in range(1, 8):
            square += w.sqb[k]
        inverse = lax.rsqrt(square / WIDTH + EPS)
        factors = [jnp.sqrt(w.sqx[k]) * (1.0 / LEVELS) * inverse for k in range(8)]
        factors = jnp.concatenate(factors + [jnp.zeros((120, padded), F32)], axis=0).T
        inverse = jnp.broadcast_to(inverse, (128, padded)).T
        for k in range(8):
            w.invc[k] = inverse[k * rows : (k + 1) * rows]
        wait_all(xz_peers, w.ub, w.s_u, w.r_u)
        for k in range(8):
            for h, part in enumerate(unpack(w.ub[k])):
                normed = part * factors[h * half : (h + 1) * half, k : k + 1] * m.gain[k : k + 1, :]
                w.ul[h * half : (h + 1) * half, k * COL : (k + 1) * COL] = normed.astype(BF16)

        def draft_step(i, carry):
            at = pl.ds(pl.multiple_of(i * 256, 256), 256)
            acc = jnp.dot(w.ul[...], m.head[:, at], preferred_element_type=F32)
            w.dd[0, :, at] = acc[:half]
            w.dd[1, :, at] = acc[half:]
            return carry

        lax.fori_loop(0, 4, draft_step, 0)
        across = copy_to(w.dd.at[1 - c], w.cr, w.s_c, w.r_c, core_dev)
        across.start()

        lane = lax.broadcasted_iota(jnp.int32, (1, 128), 1)
        valid = lane < rows
        position = sec * BLK + first + lane
        sequence = position // SPAN
        offset = position % SPAN
        length = jnp.zeros((1, 128), jnp.int32)
        keep = jnp.zeros((1, 128), jnp.int32)
        for q in range(SEQS):
            length = jnp.where(sequence == q, m.len[q], length)
            keep = jnp.where(sequence == q, m.mask[q], keep)
        live = (offset < length) & valid
        weight = jnp.where(live, keep.astype(F32) / (jnp.maximum(length, 1).astype(F32) * SEQS), 0.0)
        across.wait_recv()
        tops = []
        for k in range(4):
            at = slice(k * rows, (k + 1) * rows)
            part = w.dd[c, at, :] + w.cr[at, :]
            w.ds[k] = part
            tops.append(jnp.maximum(jnp.max(jnp.abs(part), axis=1, keepdims=True), 1e-30))
            code = part * (LEVELS / tops[-1])
            w.zs[k] = pack(code[:, : LOC // 2], code[:, LOC // 2 :])
        w.zss[...] = columns_to_rows(tops)
        send_all(zh_peers, lambda other: w.zss, w.zsr, w.s_zs, w.r_zs, zh)
        send_all(zh_peers, lambda other: w.zs.at[other], w.zr, w.s_z, w.r_z, zh)
        across.wait_send()
        draft = fold(w.ds[zh])
        target = fold(m.tl[...].astype(F32)[first : first + rows])
        yield
        wait_all(zh_peers, w.zsr, w.s_zs, w.r_zs)
        steps = rows_to_columns(stack_rows([w.zsr[other, pl.ds(zh, 1), :] for other, _ in zh_peers])) * (1.0 / LEVELS)
        wait_all(zh_peers, w.zr, w.s_z, w.r_z)
        for k, (other, _) in enumerate(zh_peers):
            draft += jnp.concatenate(unpack(w.zr[other]), axis=0) * both(steps[:rows, k : k + 1])

        def per_token(a, op, reduce):
            a = op(op(a[:, :128], a[:, 128:256]), op(a[:, 256:384], a[:, 384:]))
            return reduce(op(a[:rows], a[rows:]), axis=1, keepdims=True)

        def top(a):
            return per_token(a, jnp.maximum, jnp.max)

        def add(a):
            return per_token(a, jnp.add, jnp.sum)

        d_top = top(draft)
        d_exp = jnp.exp(draft - both(d_top))
        t_top = top(target)
        t_exp = jnp.exp(target - both(t_top))
        w.st0[...] = columns_to_rows(
            [d_top, add(d_exp), add(d_exp * draft), t_top, add(t_exp), add(t_exp * (target - draft)), add(t_exp * draft)]
        )
        send_all(xz_peers, lambda other: w.st0, w.st1, w.s_s1, w.r_s1, j)
        w.st1[j] = w.st0[...]
        yield
        wait_all(xz_peers, w.st1, w.s_s1, w.r_s1)
        w.st2[y] = stack_rows(merge_stats([w.st1[k] for k in range(8)]))
        send_all(y_peers, lambda other: w.st2.at[y], w.st2, w.s_s2, w.r_s2, y)
        yield
        wait_all(y_peers, w.st2, w.s_s2, w.r_s2)
        d_top, d_sum, d_first, t_top, t_sum, cross, t_first = merge_stats([w.st2[k] for k in range(8)])
        d_sum = jnp.where(valid, d_sum, 1.0)
        t_sum = jnp.where(valid, t_sum, 1.0)
        d_lse = d_top + jnp.log(d_sum)
        t_lse = t_top + jnp.log(t_sum)
        loss = weight * (cross / t_sum - t_lse + d_lse)
        scale = LOSS_SCALE * weight
        along = scale * (d_first / d_sum - t_first / t_sum)
        cols = rows_to_columns(stack_rows([d_lse, scale, t_top, scale / t_sum]))[:rows]
        dlogit = both(cols[:, 1:2]) * jnp.exp(draft - both(cols[:, 0:1]))
        dlogit -= both(cols[:, 3:4]) * jnp.exp(target - both(cols[:, 2:3]))
        w.dlb[pi] = dlogit.astype(BF16)
        spread(w.dlb, w.s_dl, w.r_dl, w.s_fw, w.r_fw)
        w.qb[pi] = stack_rows([along, loss])
        send_all(sec_peers, lambda other: w.qb.at[pi], w.qb, w.s_q, w.r_q, pi)
        yield
        relay(w.dlb, w.s_dl, w.r_dl, w.s_fw, w.r_fw)
        for k in range(0, 8, 2):
            pair = [unfold(w.dlb[k + i].astype(F32)) for i in range(2)]
            w.dl[k * rows : (k + 2) * rows] = jnp.concatenate(pair, axis=0).astype(BF16)

        def grad_step(i, carry):
            at = pl.ds(pl.multiple_of(i * 256, 256), 256)
            acc = lax.dot_general(w.dl[...], m.head[at, :], (((1,), (1,)), ((), ())), preferred_element_type=F32)
            w.sb2[2 * i] = acc[:, :COL].astype(BF16)
            w.sb2[2 * i + 1] = acc[:, COL:].astype(BF16)
            return carry

        lax.fori_loop(0, 4, grad_step, 0)
        yield from vocab_sum(
            from_bf16, rows, w.sb2, w.rb2, w.a2, w.b2, w.p2, w.dn, w.s_x2, w.r_x2, w.s_y2, w.r_y2, w.s_g2, w.r_g2
        )

        wait_all(sec_peers, w.qb, w.s_q, w.r_q)
        loss = w.qb[0, 1:2]
        for k in range(1, 8):
            loss += w.qb[k, 1:2]
        q_cols = rows_to_columns(stack_rows([w.qb[k, 0:1] for k in range(8)]))[:rows]
        gain = m.gain[pl.ds(j, 1), :]
        gg = jnp.zeros((rows, COL), F32)
        pair = []
        for k in range(8):
            inv = w.invc[k]
            joined = w.jy[k]
            grad = w.dn[k] * inv
            gg += grad * joined
            pair.append(grad * gain - joined * (q_cols[:, k : k + 1] * inv * inv / WIDTH))
            if k % 2:
                w.df[j, (k - 1) * rows : (k + 1) * rows] = jnp.concatenate(pair, axis=0).astype(BF16)
                pair = []
        send_all(xz_peers, lambda other: w.df.at[j], w.df, w.s_df, w.r_df, j)
        results.append((loss, jnp.sum(gg, axis=0, keepdims=True)))
        if index == len(SPLITS) - 1:
            m.ggb[j] = sum(gg for _, gg in results)
            send_all(xz_peers, lambda other: m.ggb.at[j], m.ggb, m.s_gg, m.r_gg, j)
            loss_ref[0, 0] = jnp.sum(sum(loss for loss, _ in results))
        yield
        wait_all(xz_peers, w.df, w.s_df, w.r_df)
        for k in range(8):
            grads_ref[8 * first : 8 * first + tokens, k * COL : (k + 1) * COL] = w.df[k]

    running = [chain(i) for i in range(len(SPLITS))]
    while running:
        before = len(sent)
        running = [one for one in running if next(one, running) is not running]
        settle(before)
    wait_all(xz_peers, m.ggb, m.s_gg, m.r_gg)
    for k in range(8):
        gg_ref[k : k + 1, :] = m.ggb[k]
    settle(len(sent))


def last_kernel(taps_ref, grads_ref, gg_in, loss_in, out_ref, gg_ref, loss_ref):
    out_ref[...] = lax.dot_general(
        taps_ref[...], grads_ref[...], (((0,), (0,)), ((), ())), preferred_element_type=F32
    )
    gg_ref[...] = gg_in[...]
    loss_ref[0, 0] = loss_in[0, 0]


def shards(tap_hidden, join_weight, norm_gain, head_weight, target_logits, seq_lengths, seq_mask):
    vmem = pl.BlockSpec(memory_space=pltpu.VMEM)
    smem = pl.BlockSpec(memory_space=pltpu.SMEM)
    hbm = pl.BlockSpec(memory_space=pl.ANY)
    scratch = list(shared_scratch().values())
    for rows in SPLITS:
        scratch += list(chain_scratch(rows).values())
    loss, gain_grad, taps, grads = pl.pallas_call(
        kernel,
        out_shape=(
            jax.ShapeDtypeStruct((1, 1), F32),
            jax.ShapeDtypeStruct((8, COL), F32),
            jax.ShapeDtypeStruct((TOK, TAPS * COL), BF16),
            jax.ShapeDtypeStruct((TOK, LOC), BF16),
        ),
        in_specs=[hbm] * 7,
        out_specs=(smem, vmem, vmem, vmem),
        scratch_shapes=scratch,
        compiler_params=pltpu.CompilerParams(
            collective_id=0, has_side_effects=True, vmem_limit_bytes=60 * 1024 * 1024
        ),
        name="draft_step",
    )(
        tap_hidden,
        join_weight.reshape(TAPS * COL, LOC),
        norm_gain.reshape(8, COL),
        head_weight,
        target_logits,
        seq_lengths,
        seq_mask,
    )
    tile = 256
    join_grad, gain_grad, loss = pl.pallas_call(
        last_kernel,
        grid=(LOC // tile,),
        out_shape=(
            jax.ShapeDtypeStruct((TAPS * COL, LOC), F32),
            jax.ShapeDtypeStruct((8, COL), F32),
            jax.ShapeDtypeStruct((1, 1), F32),
        ),
        in_specs=[
            pl.BlockSpec((TOK, TAPS * COL), lambda i: (0, 0)),
            pl.BlockSpec((TOK, tile), lambda i: (0, i)),
            pl.BlockSpec((8, COL), lambda i: (0, 0)),
            smem,
        ],
        out_specs=(
            pl.BlockSpec((TAPS * COL, tile), lambda i: (0, i)),
            pl.BlockSpec((8, COL), lambda i: (0, 0)),
            smem,
        ),
        compiler_params=pltpu.CompilerParams(vmem_limit_bytes=60 * 1024 * 1024),
        name="join_gradient",
    )(taps, grads, gain_grad, loss)
    return loss.reshape(()), join_grad.reshape(TAPS, COL, LOC), gain_grad.reshape(LOC)


def solution(mesh):
    in_specs = (
        P(None, "section", "vocab"),
        P(None, "vocab", "section"),
        P("section"),
        P("section", "vocab"),
        P("section", "vocab"),
        P(),
        P(),
    )
    out_specs = (P(), P(None, "vocab", "section"), P("section"))
    return jax.shard_map(shards, mesh=mesh, in_specs=in_specs, out_specs=out_specs, check_vma=False)
```

```python
import jax
import jax.numpy as jnp
from jax import lax
from jax.experimental import pallas as pl
from jax.experimental.pallas import tpu as pltpu
from jax.sharding import PartitionSpec as P

MESH = pl.DeviceIdType.MESH
F32 = jnp.float32
BF16 = jnp.bfloat16

SPAN = 32
SEQS = 10
LOSS_SCALE = 1024.0
EPS = 1e-05
WIDTH = 8192
TAPS = 3
BLK = 40
SPLITS = (16, 16, 8)
TOK = 320
COL = 128
LOC = 1024


def fold(a):
    return jnp.concatenate([a[:, : LOC // 2], a[:, LOC // 2 :]], axis=0)


def unfold(a):
    rows = a.shape[0] // 2
    return jnp.concatenate([a[:rows], a[rows:]], axis=1)


LEVELS = 32767.0
BOUND = TAPS * COL * 6.0 * 0.0390625


def pack(low, high):
    low = jnp.where(low < 0, low - 0.5, low + 0.5).astype(jnp.int32)
    high = jnp.where(high < 0, high - 0.5, high + 0.5).astype(jnp.int32)
    return (high << 16) | (low & 0xFFFF)


def unpack(word):
    return ((word << 16) >> 16).astype(F32), (word >> 16).astype(F32)


def root_code(a):
    root = jnp.sqrt(jnp.sqrt(jnp.minimum(jnp.abs(a) * (1.0 / BOUND), 1.0))) * LEVELS
    return jnp.where(a < 0, -root, root)


def root_value(code):
    code = code * (1.0 / LEVELS)
    return BOUND * (code * code) * (code * jnp.abs(code))


def both(a):
    return jnp.concatenate([a, a], axis=0)


def columns_to_rows(columns):
    rows = columns[0].shape[0]
    lane = lax.broadcasted_iota(jnp.int32, (rows, 128), 1)
    out = jnp.zeros((rows, 128), F32)
    for i, column in enumerate(columns):
        out = jnp.where(lane == i, column, out)
    out = jnp.concatenate([out, jnp.zeros((128 - rows, 128), F32)], axis=0)
    return out.T[:8]


def stack_rows(rows):
    sub = lax.broadcasted_iota(jnp.int32, (8, 128), 0)
    out = jnp.zeros((8, 128), F32)
    for i, row in enumerate(rows):
        out = jnp.where(sub == i, row, out)
    return out


def rows_to_columns(rows):
    return jnp.concatenate([rows, jnp.zeros((120, 128), F32)], axis=0).T


def merge_stats(parts):
    top_d, top_t = parts[0][0:1], parts[0][3:4]
    for p in parts[1:]:
        top_d = jnp.maximum(top_d, p[0:1])
        top_t = jnp.maximum(top_t, p[3:4])
    sums = [jnp.zeros((1, 128), F32) for _ in range(5)]
    for p in parts:
        a = jnp.exp(p[0:1] - top_d)
        b = jnp.exp(p[3:4] - top_t)
        sums[0] += a * p[1:2]
        sums[1] += a * p[2:3]
        sums[2] += b * p[4:5]
        sums[3] += b * p[5:6]
        sums[4] += b * p[6:7]
    return [top_d, sums[0], sums[1], top_t, sums[2], sums[3], sums[4]]


def pad128(tokens):
    return -(-tokens // 128) * 128


def chain_scratch(rows):
    V, dma = pltpu.VMEM, pltpu.SemaphoreType.DMA
    i32 = jnp.int32
    padded = pad128(8 * rows)
    half = LOC // 2
    buffers = dict(
        tapl=V((8 * rows, TAPS * COL), BF16), tapt=V((TAPS * COL, padded), BF16), dfl=V((padded, LOC), BF16),
        sb1=V((8, 4 * rows, COL), i32), rb1=V((8, 4 * rows, COL), i32),
        a1=V((8, rows, COL), F32), b1=V((8, rows, COL), F32), p1=V((rows, COL), F32), jy=V((8, rows, COL), F32),
        sqx=V((8, 1, padded), F32), sqb=V((8, 1, padded), F32), invc=V((8, rows, COL), F32),
        ub=V((8, 4 * rows, COL), i32), ul=V((8 * rows, LOC), BF16),
        dd=V((2, 4, 4 * rows, 256), F32), cr=V((4, 4 * rows, 256), F32), ds=V((4, rows, LOC), F32),
        zs=V((4, rows, half), i32), zr=V((4, rows, half), i32), zss=V((8, 128), F32), zsr=V((4, 8, 128), F32),
        st0=V((8, 128), F32), st1=V((8, 8, 128), F32), st2=V((8, 8, 128), F32),
        dlb=V((8, 2 * rows, half), BF16), dl=V((8 * rows, LOC), BF16),
        sb2=V((8, 8 * rows, COL), BF16), rb2=V((8, 8 * rows, COL), BF16),
        a2=V((8, rows, COL), F32), b2=V((8, rows, COL), F32), p2=V((rows, COL), F32), dn=V((8, rows, COL), F32),
        df=V((8, 8 * rows, COL), BF16),
    )
    names = ("x1", "y1", "g1", "sx", "u", "sq", "s1", "s2", "x2", "y2", "g2", "df", "z", "zs", "c", "fw")
    sems = {side + name: dma for name in names for side in ("s_", "r_")}
    sems.update(s_dl=dma, r_dl=dma((4,)))
    return buffers | sems


def shared_scratch():
    V, dma = pltpu.VMEM, pltpu.SemaphoreType.DMA
    return dict(
        tap=V((TAPS, BLK, COL), BF16), jw=V((TAPS * COL, LOC), BF16), gain=V((8, COL), F32),
        head=V((LOC, LOC), BF16), tl=V((BLK, LOC), BF16),
        len=pltpu.SMEM((SEQS,), jnp.int32), mask=pltpu.SMEM((SEQS,), jnp.int32),
        tapg=V((8, 128, COL), BF16), ggb=V((8, 1, COL), F32), qb=V((8, 1, 128), F32),
        s_in=dma((7,)), s_tap=dma, r_tap=dma((4,)), s_tf=dma, r_tf=dma, s_gg=dma, r_gg=dma, s_q=dma, r_q=dma,
    )


class Names:
    def __init__(self, names, refs):
        self.__dict__.update(zip(names, refs, strict=True))


def kernel(
    tap_hbm, jw_hbm, gain_hbm, head_hbm, tl_hbm, len_hbm, mask_hbm, loss_ref, gg_ref, out_ref, *scratch
):
    names = list(shared_scratch())
    m, scratch = Names(names, scratch[: len(names)]), scratch[len(names) :]
    chains = []
    for rows in SPLITS:
        names = list(chain_scratch(rows))
        chains.append(Names(names, scratch[: len(names)]))
        scratch = scratch[len(names) :]

    sec = lax.axis_index("section")
    voc = lax.axis_index("vocab")
    zh, c = lax.div(sec, 2), lax.rem(sec, 2)
    zl, y, x = lax.div(voc, 32), lax.rem(lax.div(voc, 4), 8), lax.rem(voc, 4)
    j = zl * 4 + x
    pi = c * 4 + zh

    sec_peers = []
    for a, b in ((2, 0), (2, 1), (1, 0), (3, 0), (1, 1), (3, 1), (0, 1)):
        zh2, c2 = lax.rem(zh + a, 4), lax.rem(c + b, 2)
        sec_peers.append((c2 * 4 + zh2, (zh2 * 2 + c2, voc)))
    zh_peers = []
    for a in (2, 1, 3):
        zh2 = lax.rem(zh + a, 4)
        zh_peers.append((zh2, (zh2 * 2 + c, voc)))
    near_first = zh_peers[1:] + zh_peers[:1]
    core_dev = (zh * 2 + (1 - c), voc)
    xz_peers = []
    for a, b in ((1, 2), (1, 1), (1, 3), (0, 2), (0, 1), (0, 3), (1, 0)):
        zl2, x2 = lax.rem(zl + a, 2), lax.rem(x + b, 4)
        xz_peers.append((zl2 * 4 + x2, (sec, zl2 * 32 + y * 4 + x2)))
    y_peers = []
    for a in (4, 3, 5, 2, 6, 1, 7):
        y2 = lax.rem(y + a, 8)
        y_peers.append((y2, (sec, zl * 32 + y2 * 4 + x)))

    inputs = (
        (tap_hbm, m.tap), (jw_hbm, m.jw), (gain_hbm, m.gain), (len_hbm, m.len), (mask_hbm, m.mask),
        (head_hbm, m.head), (tl_hbm, m.tl),
    )
    loads = [pltpu.make_async_copy(src, dst, m.s_in.at[i]) for i, (src, dst) in enumerate(inputs)]
    for load in loads:
        load.start()

    barrier = pltpu.get_barrier_semaphore()
    for _, dev in sec_peers + xz_peers + y_peers:
        pl.semaphore_signal(barrier, inc=1, device_id=dev, device_id_type=MESH)
    loads[0].wait()
    taps = [m.tap[k].astype(F32) for k in range(TAPS)] + [jnp.zeros((128 - TAPS * BLK, COL), F32)]
    m.tapg[pi] = jnp.concatenate(taps, axis=0).astype(BF16)
    pl.semaphore_wait(barrier, 21)

    def copy_to(src, dst, s_sem, r_sem, dev):
        return pltpu.make_async_remote_copy(src, dst, s_sem, r_sem, device_id=dev, device_id_type=MESH)

    sent = []

    def send_all(peers, src, dst, s_sem, r_sem, slot):
        for other, dev in peers:
            copy_to(src(other), dst.at[slot], s_sem, r_sem, dev).start()
        whole = dst.at[pl.ds(0, len(peers))]
        sent.append(copy_to(whole, whole, s_sem, r_sem, peers[0][1]))

    def settle(first):
        for copy in sent[:first]:
            copy.wait_send()
        del sent[:first]

    def wait_all(peers, dst, s_sem, r_sem):
        whole = dst.at[pl.ds(0, len(peers))]
        copy_to(whole, whole, s_sem, r_sem, peers[0][1]).wait_recv()

    def spread(buf, s_near, r_near, s_core, r_core):
        for other, dev in zh_peers:
            copy_to(buf.at[pi], buf.at[pi], s_near, r_near.at[zh], dev).start()
        copy_to(buf.at[pi], buf.at[pi], s_core, r_core, core_dev).start()

    def relay(buf, s_near, r_near, s_core, r_core):
        for other, dev in near_first:
            slot = c * 4 + other
            copy_to(buf.at[slot], buf.at[slot], s_near, r_near.at[other], dev).wait_recv()
            copy_to(buf.at[slot], buf.at[slot], s_core, r_core, core_dev).start()
        three, four = buf.at[pl.ds(0, 3)], buf.at[pl.ds(0, 4)]
        copy_to(three, three, s_near, r_near.at[0], core_dev).wait_send()
        last = copy_to(four, four, s_core, r_core, core_dev)
        last.wait_recv()
        sent.append(last)

    spread(m.tapg, m.s_tap, m.r_tap, m.s_tf, m.r_tf)
    for load in loads[1:]:
        load.wait()
    relay(m.tapg, m.s_tap, m.r_tap, m.s_tf, m.r_tf)

    def from_roots(rb):
        low, high = [root_value(half) for half in unpack(rb[0])]
        for k in range(1, 8):
            more = [root_value(half) for half in unpack(rb[k])]
            low, high = low + more[0], high + more[1]
        return jnp.concatenate([low, high], axis=0)

    def from_bf16(rb):
        total = rb[0].astype(F32)
        for k in range(1, 8):
            total += rb[k].astype(F32)
        return total

    def vocab_sum(collect, rows, sb, rb, a_buf, b_buf, p_buf, out, s_x, r_x, s_y, r_y, s_g, r_g, between=None):
        send_all(xz_peers, lambda other: sb.at[other], rb, s_x, r_x, j)
        rb[j] = sb[j]
        if between is not None:
            between()
        yield
        wait_all(xz_peers, rb, s_x, r_x)
        total = collect(rb)
        for k in range(8):
            a_buf[k] = total[k * rows : (k + 1) * rows]
        send_all(y_peers, lambda other: a_buf.at[other], b_buf, s_y, r_y, y)
        b_buf[y] = a_buf[y]
        yield
        wait_all(y_peers, b_buf, s_y, r_y)
        piece = b_buf[0]
        for k in range(1, 8):
            piece += b_buf[k]
        p_buf[...] = piece
        send_all(y_peers, lambda other: p_buf, out, s_g, r_g, y)
        out[y] = piece
        yield
        wait_all(y_peers, out, s_g, r_g)

    gain_rows = []
    per_token_rows = []

    def chain(index):
        w = chains[index]
        rows, first = SPLITS[index], sum(SPLITS[:index])
        half, tokens = 4 * rows, 8 * rows
        padded = pad128(tokens)

        blocks = [m.tapg[p].astype(F32) for p in range(8)]
        for k in range(TAPS):
            at = k * BLK + first
            tap = jnp.concatenate([b[at : at + rows] for b in blocks], axis=0)
            w.tapl[:, k * COL : (k + 1) * COL] = tap.astype(BF16)

        def join_step(i, carry):
            at = pl.ds(pl.multiple_of(i * 256, 256), 256)
            acc = root_code(jnp.dot(w.tapl[...], m.jw[:, at], preferred_element_type=F32))
            w.sb1[2 * i] = pack(acc[:half, :COL], acc[half:, :COL])
            w.sb1[2 * i + 1] = pack(acc[:half, COL:], acc[half:, COL:])
            return carry

        lax.fori_loop(0, 4, join_step, 0)

        def turn_taps():
            for k in range(TAPS):
                tap = w.tapl[:, k * COL : (k + 1) * COL].astype(F32)
                if padded > tokens:
                    tap = jnp.concatenate([tap, jnp.zeros((padded - tokens, COL), F32)], axis=0)
                w.tapt[k * COL : (k + 1) * COL, :] = tap.T.astype(BF16)
            if padded > tokens:
                w.dfl[tokens:, :] = jnp.zeros((padded - tokens, LOC), BF16)

        yield from vocab_sum(
            from_roots, rows, w.sb1, w.rb1, w.a1, w.b1, w.p1, w.jy, w.s_x1, w.r_x1, w.s_y1, w.r_y1, w.s_g1, w.r_g1,
            between=turn_taps,
        )

        joined = jnp.concatenate([w.jy[k] for k in range(8)], axis=0)
        square = joined * joined
        tall = square
        if padded > tokens:
            tall = jnp.concatenate([square, jnp.zeros((padded - tokens, COL), F32)], axis=0)
        w.sqx[j] = jnp.sum(tall.T, axis=0, keepdims=True)
        send_all(xz_peers, lambda other: w.sqx.at[j], w.sqx, w.s_sx, w.r_sx, j)
        code = joined * (LEVELS * lax.rsqrt(jnp.maximum(jnp.sum(square, axis=1, keepdims=True), 1e-30)))
        w.ub[j] = pack(code[:half], code[half:])
        send_all(xz_peers, lambda other: w.ub.at[j], w.ub, w.s_u, w.r_u, j)
        yield
        wait_all(xz_peers, w.sqx, w.s_sx, w.r_sx)
        square = w.sqx[0]
        for k in range(1, 8):
            square += w.sqx[k]
        w.sqb[pi] = square
        send_all(sec_peers, lambda other: w.sqb.at[pi], w.sqb, w.s_sq, w.r_sq, pi)
        yield
        wait_all(sec_peers, w.sqb, w.s_sq, w.r_sq)
        square = w.sqb[0]
        for k in range(1, 8):
            square += w.sqb[k]
        inverse = lax.rsqrt(square / WIDTH + EPS)
        factors = [jnp.sqrt(w.sqx[k]) * (1.0 / LEVELS) * inverse for k in range(8)]
        factors = jnp.concatenate(factors + [jnp.zeros((120, padded), F32)], axis=0).T
        inverse = jnp.broadcast_to(inverse, (128, padded)).T
        for k in range(8):
            w.invc[k] = inverse[k * rows : (k + 1) * rows]
        wait_all(xz_peers, w.ub, w.s_u, w.r_u)
        for k in range(8):
            for h, part in enumerate(unpack(w.ub[k])):
                normed = part * factors[h * half : (h + 1) * half, k : k + 1] * m.gain[k : k + 1, :]
                w.ul[h * half : (h + 1) * half, k * COL : (k + 1) * COL] = normed.astype(BF16)

        def draft_step(i, carry):
            at = pl.ds(pl.multiple_of(i * 256, 256), 256)
            acc = jnp.dot(w.ul[...], m.head[:, at], preferred_element_type=F32)
            w.dd[0, i] = acc[:half]
            w.dd[1, i] = acc[half:]
            copy_to(w.dd.at[1 - c, i], w.cr.at[i], w.s_c, w.r_c, core_dev).start()
            return carry

        lax.fori_loop(0, 4, draft_step, 0)
        across = copy_to(w.cr, w.cr, w.s_c, w.r_c, core_dev)

        lane = lax.broadcasted_iota(jnp.int32, (1, 128), 1)
        valid = lane < rows
        position = sec * BLK + first + lane
        sequence = position // SPAN
        offset = position % SPAN
        length = jnp.zeros((1, 128), jnp.int32)
        keep = jnp.zeros((1, 128), jnp.int32)
        for q in range(SEQS):
            length = jnp.where(sequence == q, m.len[q], length)
            keep = jnp.where(sequence == q, m.mask[q], keep)
        live = (offset < length) & valid
        weight = jnp.where(live, keep.astype(F32) / (jnp.maximum(length, 1).astype(F32) * SEQS), 0.0)
        across.wait_recv()
        tops = []
        for k in range(4):
            at = slice(k * rows, (k + 1) * rows)
            part = jnp.concatenate([w.dd[c, i, at, :] + w.cr[i, at, :] for i in range(4)], axis=1)
            w.ds[k] = part
            tops.append(jnp.maximum(jnp.max(jnp.abs(part), axis=1, keepdims=True), 1e-30))
            code = part * (LEVELS / tops[-1])
            w.zs[k] = pack(code[:, : LOC // 2], code[:, LOC // 2 :])
        w.zss[...] = columns_to_rows(tops)
        send_all(zh_peers, lambda other: w.zss, w.zsr, w.s_zs, w.r_zs, zh)
        send_all(zh_peers, lambda other: w.zs.at[other], w.zr, w.s_z, w.r_z, zh)
        across.wait_send()
        draft = fold(w.ds[zh])
        target = fold(m.tl[...].astype(F32)[first : first + rows])
        yield
        wait_all(zh_peers, w.zsr, w.s_zs, w.r_zs)
        steps = rows_to_columns(stack_rows([w.zsr[other, pl.ds(zh, 1), :] for other, _ in zh_peers])) * (1.0 / LEVELS)
        wait_all(zh_peers, w.zr, w.s_z, w.r_z)
        for k, (other, _) in enumerate(zh_peers):
            draft += jnp.concatenate(unpack(w.zr[other]), axis=0) * both(steps[:rows, k : k + 1])

        def per_token(a, op, reduce):
            a = op(op(a[:, :128], a[:, 128:256]), op(a[:, 256:384], a[:, 384:]))
            return reduce(op(a[:rows], a[rows:]), axis=1, keepdims=True)

        def top(a):
            return per_token(a, jnp.maximum, jnp.max)

        def add(a):
            return per_token(a, jnp.add, jnp.sum)

        d_top = top(draft)
        d_exp = jnp.exp(draft - both(d_top))
        t_top = top(target)
        t_exp = jnp.exp(target - both(t_top))
        w.st0[...] = columns_to_rows(
            [d_top, add(d_exp), add(d_exp * draft), t_top, add(t_exp), add(t_exp * (target - draft)), add(t_exp * draft)]
        )
        send_all(xz_peers, lambda other: w.st0, w.st1, w.s_s1, w.r_s1, j)
        w.st1[j] = w.st0[...]
        yield
        wait_all(xz_peers, w.st1, w.s_s1, w.r_s1)
        w.st2[y] = stack_rows(merge_stats([w.st1[k] for k in range(8)]))
        send_all(y_peers, lambda other: w.st2.at[y], w.st2, w.s_s2, w.r_s2, y)
        yield
        wait_all(y_peers, w.st2, w.s_s2, w.r_s2)
        d_top, d_sum, d_first, t_top, t_sum, cross, t_first = merge_stats([w.st2[k] for k in range(8)])
        d_sum = jnp.where(valid, d_sum, 1.0)
        t_sum = jnp.where(valid, t_sum, 1.0)
        d_lse = d_top + jnp.log(d_sum)
        t_lse = t_top + jnp.log(t_sum)
        loss = weight * (cross / t_sum - t_lse + d_lse)
        scale = LOSS_SCALE * weight
        along = scale * (d_first / d_sum - t_first / t_sum)
        cols = rows_to_columns(stack_rows([d_lse, scale, t_top, scale / t_sum]))[:rows]
        dlogit = both(cols[:, 1:2]) * jnp.exp(draft - both(cols[:, 0:1]))
        dlogit -= both(cols[:, 3:4]) * jnp.exp(target - both(cols[:, 2:3]))
        w.dlb[pi] = dlogit.astype(BF16)
        spread(w.dlb, w.s_dl, w.r_dl, w.s_fw, w.r_fw)
        for row, at in ((along, first), (loss, first + 64)):
            row = jnp.broadcast_to(row, (8, 128))
            per_token_rows.append((pltpu.roll(row, at, 1) if at else row)[0:1])
        if index == len(SPLITS) - 1:
            m.qb[pi] = sum(per_token_rows)
            send_all(sec_peers, lambda other: m.qb.at[pi], m.qb, m.s_q, m.r_q, pi)
        yield
        relay(w.dlb, w.s_dl, w.r_dl, w.s_fw, w.r_fw)
        for k in range(0, 8, 2):
            pair = [unfold(w.dlb[k + i].astype(F32)) for i in range(2)]
            w.dl[k * rows : (k + 2) * rows] = jnp.concatenate(pair, axis=0).astype(BF16)

        def grad_step(i, carry):
            at = pl.ds(pl.multiple_of(i * 256, 256), 256)
            acc = lax.dot_general(w.dl[...], m.head[at, :], (((1,), (1,)), ((), ())), preferred_element_type=F32)
            w.sb2[2 * i] = acc[:, :COL].astype(BF16)
            w.sb2[2 * i + 1] = acc[:, COL:].astype(BF16)
            return carry

        lax.fori_loop(0, 4, grad_step, 0)
        yield from vocab_sum(
            from_bf16, rows, w.sb2, w.rb2, w.a2, w.b2, w.p2, w.dn, w.s_x2, w.r_x2, w.s_y2, w.r_y2, w.s_g2, w.r_g2
        )

        if index == 0:
            wait_all(sec_peers, m.qb, m.s_q, m.r_q)
            gathered = m.qb[0]
            for k in range(1, 8):
                gathered += m.qb[k]
            loss_ref[0, 0] = jnp.sum(jnp.where(lax.broadcasted_iota(jnp.int32, (1, 128), 1) < 64, 0.0, gathered))
        q_cols = rows_to_columns(stack_rows([m.qb[k] for k in range(8)]))[first : first + rows]
        gain = m.gain[pl.ds(j, 1), :]
        gg = jnp.zeros((rows, COL), F32)
        pair = []
        for k in range(8):
            inv = w.invc[k]
            joined = w.jy[k]
            grad = w.dn[k] * inv
            gg += grad * joined
            pair.append(grad * gain - joined * (q_cols[:, k : k + 1] * inv * inv / WIDTH))
            if k % 2:
                w.df[j, (k - 1) * rows : (k + 1) * rows] = jnp.concatenate(pair, axis=0).astype(BF16)
                pair = []
        send_all(xz_peers, lambda other: w.df.at[j], w.df, w.s_df, w.r_df, j)
        gain_rows.append(jnp.sum(gg, axis=0, keepdims=True))
        if index == len(SPLITS) - 1:
            m.ggb[j] = sum(gain_rows)
            send_all(xz_peers, lambda other: m.ggb.at[j], m.ggb, m.s_gg, m.r_gg, j)
        yield
        wait_all(xz_peers, w.df, w.s_df, w.r_df)
        for k in range(8):
            w.dfl[:tokens, k * COL : (k + 1) * COL] = w.df[k]

        def out_step(i, carry):
            at = pl.ds(pl.multiple_of(i * 256, 256), 256)
            part = jnp.dot(w.tapt[...], w.dfl[:, at], preferred_element_type=F32)
            out_ref[:, at] = part if index == 0 else out_ref[:, at] + part
            return carry

        lax.fori_loop(0, 4, out_step, 0)

    running = [chain(i) for i in range(len(SPLITS))]
    while running:
        before = len(sent)
        running = [one for one in running if next(one, running) is not running]
        settle(before)
    wait_all(xz_peers, m.ggb, m.s_gg, m.r_gg)
    for k in range(8):
        gg_ref[k : k + 1, :] = m.ggb[k]
    settle(len(sent))


def shards(tap_hidden, join_weight, norm_gain, head_weight, target_logits, seq_lengths, seq_mask):
    vmem = pl.BlockSpec(memory_space=pltpu.VMEM)
    smem = pl.BlockSpec(memory_space=pltpu.SMEM)
    hbm = pl.BlockSpec(memory_space=pl.ANY)
    scratch = list(shared_scratch().values())
    for rows in SPLITS:
        scratch += list(chain_scratch(rows).values())
    inputs = (
        tap_hidden,
        join_weight.reshape(TAPS * COL, LOC),
        norm_gain.reshape(8, COL),
        head_weight,
        target_logits,
        seq_lengths,
        seq_mask,
    )
    loss, gain_grad, join_grad = pl.pallas_call(
        kernel,
        out_shape=(
            jax.ShapeDtypeStruct((1, 1), F32),
            jax.ShapeDtypeStruct((8, COL), F32),
            jax.ShapeDtypeStruct((TAPS * COL, LOC), F32),
        ),
        in_specs=[hbm] * 7,
        out_specs=(smem, vmem, vmem),
        scratch_shapes=scratch,
        compiler_params=pltpu.CompilerParams(
            collective_id=0, has_side_effects=True, vmem_limit_bytes=40 * 1024 * 1024
        ),
        name="draft_step",
    )(*[pltpu.with_memory_space_constraint(a, pltpu.HBM) for a in inputs])
    return loss.reshape(()), join_grad.reshape(TAPS, COL, LOC), gain_grad.reshape(LOC)


def solution(mesh):
    in_specs = (
        P(None, "section", "vocab"),
        P(None, "vocab", "section"),
        P("section"),
        P("section", "vocab"),
        P("section", "vocab"),
        P(),
        P(),
    )
    out_specs = (P(), P(None, "vocab", "section"), P("section"))
    return jax.shard_map(shards, mesh=mesh, in_specs=in_specs, out_specs=out_specs, check_vma=False)
```

```python
import jax
import jax.numpy as jnp
from jax import lax
from jax.experimental import pallas as pl
from jax.experimental.pallas import tpu as pltpu
from jax.sharding import PartitionSpec as P

MESH = pl.DeviceIdType.MESH
F32 = jnp.float32
BF16 = jnp.bfloat16

SPAN = 32
SEQS = 10
LOSS_SCALE = 1024.0
EPS = 1e-05
WIDTH = 8192
TAPS = 3
BLK = 40
SPLITS = (16, 16, 8)
TOK = 320
COL = 128
LOC = 1024


def fold(a):
    return jnp.concatenate([a[:, : LOC // 2], a[:, LOC // 2 :]], axis=0)


def unfold(a):
    rows = a.shape[0] // 2
    return jnp.concatenate([a[:rows], a[rows:]], axis=1)


LEVELS = 32767.0
BOUND = TAPS * COL * 6.0 * 0.0390625


def pack(low, high):
    low = jnp.where(low < 0, low - 0.5, low + 0.5).astype(jnp.int32)
    high = jnp.where(high < 0, high - 0.5, high + 0.5).astype(jnp.int32)
    return (high << 16) | (low & 0xFFFF)


def unpack(word):
    return ((word << 16) >> 16).astype(F32), (word >> 16).astype(F32)


def root_code(a):
    root = jnp.sqrt(jnp.sqrt(jnp.minimum(jnp.abs(a) * (1.0 / BOUND), 1.0))) * LEVELS
    return jnp.where(a < 0, -root, root)


def root_value(code):
    code = code * (1.0 / LEVELS)
    return BOUND * (code * code) * (code * jnp.abs(code))


def both(a):
    return jnp.concatenate([a, a], axis=0)


def columns_to_rows(columns):
    rows = columns[0].shape[0]
    lane = lax.broadcasted_iota(jnp.int32, (rows, 128), 1)
    out = jnp.zeros((rows, 128), F32)
    for i, column in enumerate(columns):
        out = jnp.where(lane == i, column, out)
    out = jnp.concatenate([out, jnp.zeros((128 - rows, 128), F32)], axis=0)
    return out.T[:8]


def stack_rows(rows):
    sub = lax.broadcasted_iota(jnp.int32, (8, 128), 0)
    out = jnp.zeros((8, 128), F32)
    for i, row in enumerate(rows):
        out = jnp.where(sub == i, row, out)
    return out


def rows_to_columns(rows):
    return jnp.concatenate([rows, jnp.zeros((120, 128), F32)], axis=0).T


def merge_stats(parts):
    top_d, top_t = parts[0][0:1], parts[0][3:4]
    for p in parts[1:]:
        top_d = jnp.maximum(top_d, p[0:1])
        top_t = jnp.maximum(top_t, p[3:4])
    sums = [jnp.zeros((1, 128), F32) for _ in range(5)]
    for p in parts:
        a = jnp.exp(p[0:1] - top_d)
        b = jnp.exp(p[3:4] - top_t)
        sums[0] += a * p[1:2]
        sums[1] += a * p[2:3]
        sums[2] += b * p[4:5]
        sums[3] += b * p[5:6]
        sums[4] += b * p[6:7]
    return [top_d, sums[0], sums[1], top_t, sums[2], sums[3], sums[4]]


def pad128(tokens):
    return -(-tokens // 128) * 128


def tap_rows(rows):
    return -(-TAPS * rows // 16) * 16


def chain_scratch(rows):
    V, dma = pltpu.VMEM, pltpu.SemaphoreType.DMA
    i32 = jnp.int32
    padded = pad128(8 * rows)
    half = LOC // 2
    buffers = dict(
        tapg=V((8, tap_rows(rows), COL), BF16), tapl=V((8 * rows, TAPS * COL), BF16), tapt=V((TAPS * COL, padded), BF16), dfl=V((padded, LOC), BF16),
        sb1=V((8, 4 * rows, COL), i32), rb1=V((8, 4 * rows, COL), i32),
        a1=V((8, rows, COL), F32), b1=V((8, rows, COL), F32), p1=V((rows, COL), F32), jy=V((8, rows, COL), F32),
        sqx=V((8, 1, padded), F32), sqb=V((8, 1, padded), F32), invc=V((8, rows, COL), F32),
        ub=V((8, 4 * rows, COL), i32), ul=V((8 * rows, LOC), BF16),
        dd=V((2, 4, 4 * rows, 256), F32), cr=V((4, 4 * rows, 256), F32), ds=V((4, rows, LOC), F32),
        zs=V((4, rows, half), i32), zr=V((4, rows, half), i32), zss=V((8, 128), F32), zsr=V((4, 8, 128), F32),
        st0=V((8, 128), F32), st1=V((8, 8, 128), F32), st2=V((8, 8, 128), F32),
        dlb=V((8, 2 * rows, half), BF16), dl=V((8 * rows, LOC), BF16),
        sb2=V((8, 8 * rows, COL), BF16), rb2=V((8, 8 * rows, COL), BF16),
        a2=V((8, rows, COL), F32), b2=V((8, rows, COL), F32), p2=V((rows, COL), F32), dn=V((8, rows, COL), F32),
        df=V((8, 8 * rows, COL), BF16),
    )
    names = ("x1", "y1", "g1", "sx", "u", "sq", "s1", "s2", "x2", "y2", "g2", "df", "z", "zs", "c", "fw", "tf")
    sems = {side + name: dma for name in names for side in ("s_", "r_")}
    sems.update(s_dl=dma, r_dl=dma((4,)), s_tap=dma, r_tap=dma((4,)))
    return buffers | sems


def shared_scratch():
    V, dma = pltpu.VMEM, pltpu.SemaphoreType.DMA
    return dict(
        tap=V((TAPS, BLK, COL), BF16), jw=V((TAPS * COL, LOC), BF16), gain=V((8, COL), F32),
        head=V((LOC, LOC), BF16), tl=V((BLK, LOC), BF16),
        len=pltpu.SMEM((SEQS,), jnp.int32), mask=pltpu.SMEM((SEQS,), jnp.int32),
        ggb=V((8, 1, COL), F32), qb=V((8, 1, 128), F32),
        s_in=dma((7,)), s_gg=dma, r_gg=dma, s_q=dma, r_q=dma,
    )


class Names:
    def __init__(self, names, refs):
        self.__dict__.update(zip(names, refs, strict=True))


def kernel(
    tap_hbm, jw_hbm, gain_hbm, head_hbm, tl_hbm, len_hbm, mask_hbm, loss_ref, gg_ref, out_ref, *scratch
):
    names = list(shared_scratch())
    m, scratch = Names(names, scratch[: len(names)]), scratch[len(names) :]
    chains = []
    for rows in SPLITS:
        names = list(chain_scratch(rows))
        chains.append(Names(names, scratch[: len(names)]))
        scratch = scratch[len(names) :]

    sec = lax.axis_index("section")
    voc = lax.axis_index("vocab")
    zh, c = lax.div(sec, 2), lax.rem(sec, 2)
    zl, y, x = lax.div(voc, 32), lax.rem(lax.div(voc, 4), 8), lax.rem(voc, 4)
    j = zl * 4 + x
    pi = c * 4 + zh

    sec_peers = []
    for a, b in ((2, 0), (2, 1), (1, 0), (3, 0), (1, 1), (3, 1), (0, 1)):
        zh2, c2 = lax.rem(zh + a, 4), lax.rem(c + b, 2)
        sec_peers.append((c2 * 4 + zh2, (zh2 * 2 + c2, voc)))
    zh_peers = []
    for a in (2, 1, 3):
        zh2 = lax.rem(zh + a, 4)
        zh_peers.append((zh2, (zh2 * 2 + c, voc)))
    near_first = zh_peers[1:] + zh_peers[:1]
    core_dev = (zh * 2 + (1 - c), voc)
    xz_peers = []
    for a, b in ((1, 2), (1, 1), (1, 3), (0, 2), (0, 1), (0, 3), (1, 0)):
        zl2, x2 = lax.rem(zl + a, 2), lax.rem(x + b, 4)
        xz_peers.append((zl2 * 4 + x2, (sec, zl2 * 32 + y * 4 + x2)))
    y_peers = []
    for a in (4, 3, 5, 2, 6, 1, 7):
        y2 = lax.rem(y + a, 8)
        y_peers.append((y2, (sec, zl * 32 + y2 * 4 + x)))

    inputs = (
        (tap_hbm, m.tap), (jw_hbm, m.jw), (gain_hbm, m.gain), (len_hbm, m.len), (mask_hbm, m.mask),
        (head_hbm, m.head), (tl_hbm, m.tl),
    )
    loads = [pltpu.make_async_copy(src, dst, m.s_in.at[i]) for i, (src, dst) in enumerate(inputs)]
    for load in loads:
        load.start()

    barrier = pltpu.get_barrier_semaphore()
    for _, dev in sec_peers + xz_peers + y_peers:
        pl.semaphore_signal(barrier, inc=1, device_id=dev, device_id_type=MESH)
    loads[0].wait()
    taps = [m.tap[k].astype(F32) for k in range(TAPS)]
    for i, rows in enumerate(SPLITS):
        first = sum(SPLITS[:i])
        parts = [tap[first : first + rows] for tap in taps]
        if tap_rows(rows) > TAPS * rows:
            parts.append(jnp.zeros((tap_rows(rows) - TAPS * rows, COL), F32))
        chains[i].tapg[pi] = jnp.concatenate(parts, axis=0).astype(BF16)
    pl.semaphore_wait(barrier, 21)

    def copy_to(src, dst, s_sem, r_sem, dev):
        return pltpu.make_async_remote_copy(src, dst, s_sem, r_sem, device_id=dev, device_id_type=MESH)

    sent = []

    def send_all(peers, src, dst, s_sem, r_sem, slot):
        for other, dev in peers:
            copy_to(src(other), dst.at[slot], s_sem, r_sem, dev).start()
        whole = dst.at[pl.ds(0, len(peers))]
        sent.append(copy_to(whole, whole, s_sem, r_sem, peers[0][1]))

    def settle(first):
        for copy in sent[:first]:
            copy.wait_send()
        del sent[:first]

    def wait_all(peers, dst, s_sem, r_sem):
        whole = dst.at[pl.ds(0, len(peers))]
        copy_to(whole, whole, s_sem, r_sem, peers[0][1]).wait_recv()

    def spread(buf, s_near, r_near, s_core, r_core):
        for other, dev in zh_peers:
            copy_to(buf.at[pi], buf.at[pi], s_near, r_near.at[zh], dev).start()
        copy_to(buf.at[pi], buf.at[pi], s_core, r_core, core_dev).start()

    def relay(buf, s_near, r_near, s_core, r_core):
        for other, dev in near_first:
            slot = c * 4 + other
            copy_to(buf.at[slot], buf.at[slot], s_near, r_near.at[other], dev).wait_recv()
            copy_to(buf.at[slot], buf.at[slot], s_core, r_core, core_dev).start()
        three, four = buf.at[pl.ds(0, 3)], buf.at[pl.ds(0, 4)]
        copy_to(three, three, s_near, r_near.at[0], core_dev).wait_send()
        last = copy_to(four, four, s_core, r_core, core_dev)
        last.wait_recv()
        sent.append(last)

    for w in chains:
        spread(w.tapg, w.s_tap, w.r_tap, w.s_tf, w.r_tf)
    for load in loads[1:]:
        load.wait()

    def send_two(tile, sb, rb, s_x, r_x):
        for other in (2 * tile, 2 * tile + 1):
            dev = (sec, lax.div(other, 4) * 32 + y * 4 + lax.rem(other, 4))

            @pl.when(other != j)
            def _():
                copy_to(sb.at[other], rb.at[j], s_x, r_x, dev).start()

    def from_roots(rb):
        low, high = [root_value(half) for half in unpack(rb[0])]
        for k in range(1, 8):
            more = [root_value(half) for half in unpack(rb[k])]
            low, high = low + more[0], high + more[1]
        return jnp.concatenate([low, high], axis=0)

    def from_bf16(rb):
        total = rb[0].astype(F32)
        for k in range(1, 8):
            total += rb[k].astype(F32)
        return total

    def vocab_sum(collect, rows, sb, rb, a_buf, b_buf, p_buf, out, s_x, r_x, s_y, r_y, s_g, r_g, between=None):
        whole = rb.at[pl.ds(0, 7)]
        sent.append(copy_to(whole, whole, s_x, r_x, xz_peers[0][1]))
        rb[j] = sb[j]
        if between is not None:
            between()
        yield
        wait_all(xz_peers, rb, s_x, r_x)
        total = collect(rb)
        for k in range(8):
            a_buf[k] = total[k * rows : (k + 1) * rows]
        send_all(y_peers, lambda other: a_buf.at[other], b_buf, s_y, r_y, y)
        b_buf[y] = a_buf[y]
        yield
        wait_all(y_peers, b_buf, s_y, r_y)
        piece = b_buf[0]
        for k in range(1, 8):
            piece += b_buf[k]
        p_buf[...] = piece
        send_all(y_peers, lambda other: p_buf, out, s_g, r_g, y)
        out[y] = piece
        yield
        wait_all(y_peers, out, s_g, r_g)

    gain_rows = []
    per_token_rows = []

    def chain(index):
        w = chains[index]
        rows, first = SPLITS[index], sum(SPLITS[:index])
        half, tokens = 4 * rows, 8 * rows
        padded = pad128(tokens)

        relay(w.tapg, w.s_tap, w.r_tap, w.s_tf, w.r_tf)
        blocks = [w.tapg[p].astype(F32) for p in range(8)]
        for k in range(TAPS):
            tap = jnp.concatenate([b[k * rows : (k + 1) * rows] for b in blocks], axis=0)
            w.tapl[:, k * COL : (k + 1) * COL] = tap.astype(BF16)

        def join_step(i, carry):
            i = lax.rem(i + lax.div(j, 2) + 1, 4)
            at = pl.ds(pl.multiple_of(i * 256, 256), 256)
            acc = root_code(jnp.dot(w.tapl[...], m.jw[:, at], preferred_element_type=F32))
            w.sb1[2 * i] = pack(acc[:half, :COL], acc[half:, :COL])
            w.sb1[2 * i + 1] = pack(acc[:half, COL:], acc[half:, COL:])
            send_two(i, w.sb1, w.rb1, w.s_x1, w.r_x1)
            return carry

        lax.fori_loop(0, 4, join_step, 0)

        def turn_taps():
            for k in range(TAPS):
                tap = w.tapl[:, k * COL : (k + 1) * COL].astype(F32)
                if padded > tokens:
                    tap = jnp.concatenate([tap, jnp.zeros((padded - tokens, COL), F32)], axis=0)
                w.tapt[k * COL : (k + 1) * COL, :] = tap.T.astype(BF16)
            if padded > tokens:
                w.dfl[tokens:, :] = jnp.zeros((padded - tokens, LOC), BF16)

        yield from vocab_sum(
            from_roots, rows, w.sb1, w.rb1, w.a1, w.b1, w.p1, w.jy, w.s_x1, w.r_x1, w.s_y1, w.r_y1, w.s_g1, w.r_g1,
            between=turn_taps,
        )

        joined = jnp.concatenate([w.jy[k] for k in range(8)], axis=0)
        square = joined * joined
        tall = square
        if padded > tokens:
            tall = jnp.concatenate([square, jnp.zeros((padded - tokens, COL), F32)], axis=0)
        w.sqx[j] = jnp.sum(tall.T, axis=0, keepdims=True)
        send_all(xz_peers, lambda other: w.sqx.at[j], w.sqx, w.s_sx, w.r_sx, j)
        code = joined * (LEVELS * lax.rsqrt(jnp.maximum(jnp.sum(square, axis=1, keepdims=True), 1e-30)))
        w.ub[j] = pack(code[:half], code[half:])
        send_all(xz_peers, lambda other: w.ub.at[j], w.ub, w.s_u, w.r_u, j)
        yield
        wait_all(xz_peers, w.sqx, w.s_sx, w.r_sx)
        square = w.sqx[0]
        for k in range(1, 8):
            square += w.sqx[k]
        w.sqb[pi] = square
        send_all(sec_peers, lambda other: w.sqb.at[pi], w.sqb, w.s_sq, w.r_sq, pi)
        yield
        wait_all(sec_peers, w.sqb, w.s_sq, w.r_sq)
        square = w.sqb[0]
        for k in range(1, 8):
            square += w.sqb[k]
        inverse = lax.rsqrt(square / WIDTH + EPS)
        factors = [jnp.sqrt(w.sqx[k]) * (1.0 / LEVELS) * inverse for k in range(8)]
        factors = jnp.concatenate(factors + [jnp.zeros((120, padded), F32)], axis=0).T
        inverse = jnp.broadcast_to(inverse, (128, padded)).T
        for k in range(8):
            w.invc[k] = inverse[k * rows : (k + 1) * rows]
        wait_all(xz_peers, w.ub, w.s_u, w.r_u)
        for k in range(8):
            for h, part in enumerate(unpack(w.ub[k])):
                normed = part * factors[h * half : (h + 1) * half, k : k + 1] * m.gain[k : k + 1, :]
                w.ul[h * half : (h + 1) * half, k * COL : (k + 1) * COL] = normed.astype(BF16)

        def draft_step(i, carry):
            at = pl.ds(pl.multiple_of(i * 256, 256), 256)
            acc = jnp.dot(w.ul[...], m.head[:, at], preferred_element_type=F32)
            w.dd[0, i] = acc[:half]
            w.dd[1, i] = acc[half:]
            copy_to(w.dd.at[1 - c, i], w.cr.at[i], w.s_c, w.r_c, core_dev).start()
            return carry

        lax.fori_loop(0, 4, draft_step, 0)
        across = copy_to(w.cr, w.cr, w.s_c, w.r_c, core_dev)

        lane = lax.broadcasted_iota(jnp.int32, (1, 128), 1)
        valid = lane < rows
        position = sec * BLK + first + lane
        sequence = position // SPAN
        offset = position % SPAN
        length = jnp.zeros((1, 128), jnp.int32)
        keep = jnp.zeros((1, 128), jnp.int32)
        for q in range(SEQS):
            length = jnp.where(sequence == q, m.len[q], length)
            keep = jnp.where(sequence == q, m.mask[q], keep)
        live = (offset < length) & valid
        weight = jnp.where(live, keep.astype(F32) / (jnp.maximum(length, 1).astype(F32) * SEQS), 0.0)
        across.wait_recv()
        tops = []
        for k in range(4):
            at = slice(k * rows, (k + 1) * rows)
            part = jnp.concatenate([w.dd[c, i, at, :] + w.cr[i, at, :] for i in range(4)], axis=1)
            w.ds[k] = part
            tops.append(jnp.maximum(jnp.max(jnp.abs(part), axis=1, keepdims=True), 1e-30))
            code = part * (LEVELS / tops[-1])
            w.zs[k] = pack(code[:, : LOC // 2], code[:, LOC // 2 :])
        w.zss[...] = columns_to_rows(tops)
        send_all(zh_peers, lambda other: w.zss, w.zsr, w.s_zs, w.r_zs, zh)
        send_all(zh_peers, lambda other: w.zs.at[other], w.zr, w.s_z, w.r_z, zh)
        across.wait_send()
        draft = fold(w.ds[zh])
        target = fold(m.tl[...].astype(F32)[first : first + rows])
        yield
        wait_all(zh_peers, w.zsr, w.s_zs, w.r_zs)
        steps = rows_to_columns(stack_rows([w.zsr[other, pl.ds(zh, 1), :] for other, _ in zh_peers])) * (1.0 / LEVELS)
        wait_all(zh_peers, w.zr, w.s_z, w.r_z)
        for k, (other, _) in enumerate(zh_peers):
            draft += jnp.concatenate(unpack(w.zr[other]), axis=0) * both(steps[:rows, k : k + 1])

        def per_token(a, op, reduce):
            a = op(op(a[:, :128], a[:, 128:256]), op(a[:, 256:384], a[:, 384:]))
            return reduce(op(a[:rows], a[rows:]), axis=1, keepdims=True)

        def top(a):
            return per_token(a, jnp.maximum, jnp.max)

        def add(a):
            return per_token(a, jnp.add, jnp.sum)

        d_top = top(draft)
        d_exp = jnp.exp(draft - both(d_top))
        t_top = top(target)
        t_exp = jnp.exp(target - both(t_top))
        w.st0[...] = columns_to_rows(
            [d_top, add(d_exp), add(d_exp * draft), t_top, add(t_exp), add(t_exp * (target - draft)), add(t_exp * draft)]
        )
        send_all(xz_peers, lambda other: w.st0, w.st1, w.s_s1, w.r_s1, j)
        w.st1[j] = w.st0[...]
        yield
        wait_all(xz_peers, w.st1, w.s_s1, w.r_s1)
        w.st2[y] = stack_rows(merge_stats([w.st1[k] for k in range(8)]))
        send_all(y_peers, lambda other: w.st2.at[y], w.st2, w.s_s2, w.r_s2, y)
        yield
        wait_all(y_peers, w.st2, w.s_s2, w.r_s2)
        d_top, d_sum, d_first, t_top, t_sum, cross, t_first = merge_stats([w.st2[k] for k in range(8)])
        d_sum = jnp.where(valid, d_sum, 1.0)
        t_sum = jnp.where(valid, t_sum, 1.0)
        d_lse = d_top + jnp.log(d_sum)
        t_lse = t_top + jnp.log(t_sum)
        loss = weight * (cross / t_sum - t_lse + d_lse)
        scale = LOSS_SCALE * weight
        along = scale * (d_first / d_sum - t_first / t_sum)
        cols = rows_to_columns(stack_rows([d_lse, scale, t_top, scale / t_sum]))[:rows]
        dlogit = both(cols[:, 1:2]) * jnp.exp(draft - both(cols[:, 0:1]))
        dlogit -= both(cols[:, 3:4]) * jnp.exp(target - both(cols[:, 2:3]))
        w.dlb[pi] = dlogit.astype(BF16)
        spread(w.dlb, w.s_dl, w.r_dl, w.s_fw, w.r_fw)
        for row, at in ((along, first), (loss, first + 64)):
            row = jnp.broadcast_to(row, (8, 128))
            per_token_rows.append((pltpu.roll(row, at, 1) if at else row)[0:1])
        if index == len(SPLITS) - 1:
            m.qb[pi] = sum(per_token_rows)
            send_all(sec_peers, lambda other: m.qb.at[pi], m.qb, m.s_q, m.r_q, pi)
        yield
        relay(w.dlb, w.s_dl, w.r_dl, w.s_fw, w.r_fw)
        for k in range(0, 8, 2):
            pair = [unfold(w.dlb[k + i].astype(F32)) for i in range(2)]
            w.dl[k * rows : (k + 2) * rows] = jnp.concatenate(pair, axis=0).astype(BF16)

        def grad_step(i, carry):
            i = lax.rem(i + lax.div(j, 2) + 1, 4)
            at = pl.ds(pl.multiple_of(i * 256, 256), 256)
            acc = lax.dot_general(w.dl[...], m.head[at, :], (((1,), (1,)), ((), ())), preferred_element_type=F32)
            w.sb2[2 * i] = acc[:, :COL].astype(BF16)
            w.sb2[2 * i + 1] = acc[:, COL:].astype(BF16)
            send_two(i, w.sb2, w.rb2, w.s_x2, w.r_x2)
            return carry

        lax.fori_loop(0, 4, grad_step, 0)
        yield from vocab_sum(
            from_bf16, rows, w.sb2, w.rb2, w.a2, w.b2, w.p2, w.dn, w.s_x2, w.r_x2, w.s_y2, w.r_y2, w.s_g2, w.r_g2
        )

        if index == 0:
            wait_all(sec_peers, m.qb, m.s_q, m.r_q)
            gathered = m.qb[0]
            for k in range(1, 8):
                gathered += m.qb[k]
            loss_ref[0, 0] = jnp.sum(jnp.where(lax.broadcasted_iota(jnp.int32, (1, 128), 1) < 64, 0.0, gathered))
        q_cols = rows_to_columns(stack_rows([m.qb[k] for k in range(8)]))[first : first + rows]
        gain = m.gain[pl.ds(j, 1), :]
        gg = jnp.zeros((rows, COL), F32)
        pair = []
        for k in range(8):
            inv = w.invc[k]
            joined = w.jy[k]
            grad = w.dn[k] * inv
            gg += grad * joined
            pair.append(grad * gain - joined * (q_cols[:, k : k + 1] * inv * inv / WIDTH))
            if k % 2:
                w.df[j, (k - 1) * rows : (k + 1) * rows] = jnp.concatenate(pair, axis=0).astype(BF16)
                pair = []
        send_all(xz_peers, lambda other: w.df.at[j], w.df, w.s_df, w.r_df, j)
        gain_rows.append(jnp.sum(gg, axis=0, keepdims=True))
        if index == len(SPLITS) - 1:
            m.ggb[j] = sum(gain_rows)
            send_all(xz_peers, lambda other: m.ggb.at[j], m.ggb, m.s_gg, m.r_gg, j)
        yield
        wait_all(xz_peers, w.df, w.s_df, w.r_df)
        for k in range(8):
            w.dfl[:tokens, k * COL : (k + 1) * COL] = w.df[k]

        def out_step(i, carry):
            at = pl.ds(pl.multiple_of(i * 256, 256), 256)
            part = jnp.dot(w.tapt[...], w.dfl[:, at], preferred_element_type=F32)
            out_ref[:, at] = part if index == 0 else out_ref[:, at] + part
            return carry

        lax.fori_loop(0, 4, out_step, 0)

    running = [chain(i) for i in range(len(SPLITS))]
    while running:
        before = len(sent)
        running = [one for one in running if next(one, running) is not running]
        settle(before)
    wait_all(xz_peers, m.ggb, m.s_gg, m.r_gg)
    for k in range(8):
        gg_ref[k : k + 1, :] = m.ggb[k]
    settle(len(sent))


def shards(tap_hidden, join_weight, norm_gain, head_weight, target_logits, seq_lengths, seq_mask):
    vmem = pl.BlockSpec(memory_space=pltpu.VMEM)
    smem = pl.BlockSpec(memory_space=pltpu.SMEM)
    hbm = pl.BlockSpec(memory_space=pl.ANY)
    scratch = list(shared_scratch().values())
    for rows in SPLITS:
        scratch += list(chain_scratch(rows).values())
    inputs = (
        tap_hidden,
        join_weight.reshape(TAPS * COL, LOC),
        norm_gain.reshape(8, COL),
        head_weight,
        target_logits,
        seq_lengths,
        seq_mask,
    )
    loss, gain_grad, join_grad = pl.pallas_call(
        kernel,
        out_shape=(
            jax.ShapeDtypeStruct((1, 1), F32),
            jax.ShapeDtypeStruct((8, COL), F32),
            jax.ShapeDtypeStruct((TAPS * COL, LOC), F32),
        ),
        in_specs=[hbm] * 7,
        out_specs=(smem, vmem, vmem),
        scratch_shapes=scratch,
        compiler_params=pltpu.CompilerParams(
            collective_id=0, has_side_effects=True, vmem_limit_bytes=40 * 1024 * 1024
        ),
        name="draft_step",
    )(*[pltpu.with_memory_space_constraint(a, pltpu.HBM) for a in inputs])
    return loss.reshape(()), join_grad.reshape(TAPS, COL, LOC), gain_grad.reshape(LOC)


def solution(mesh):
    in_specs = (
        P(None, "section", "vocab"),
        P(None, "vocab", "section"),
        P("section"),
        P("section", "vocab"),
        P("section", "vocab"),
        P(),
        P(),
    )
    out_specs = (P(), P(None, "vocab", "section"), P("section"))
    return jax.shard_map(shards, mesh=mesh, in_specs=in_specs, out_specs=out_specs, check_vma=False)
```
